32 devices in a mesh: row: 8 (over z, x), col: 2 (over core), grp: 2 (over y).
Axes of the slice: x: 2, y: 2, z: 4, core: 2. Of those that a mesh axis runs over, the one named last changes fastest.
Arguments:
- patches: bfloat16 [2, 512, 1408], P('grp', 'row', 'col'), may hold values from -6 to 6
- vis_gain: bfloat16 [1408], P('col'), may hold values from 0.25 to 1.75
- vis_bias: bfloat16 [1408], P('col'), may hold values from -3 to 3
- vis_qkv: bfloat16 [1408, 4224], P('col', 'row'), may hold values from -1 to 1
- vis_qkv_bias: bfloat16 [4224], P('row'), may hold values from -3 to 3
- vis_out: bfloat16 [1408, 1408], P('row', 'col'), may hold values from -0.15625 to 0.15625
- vis_out_bias: bfloat16 [1408], P('col'), may hold values from -3 to 3
- proj_weight: bfloat16 [4, 1408, 1408], P(None, 'col', 'row'), may hold values from -0.078125 to 0.078125
- proj_bias: bfloat16 [1408], P('row'), may hold values from -3 to 3
- text_embeds: bfloat16 [2, 2048, 1408], P('grp', 'col', 'row'), may hold values from -6 to 6
- dec_gain: bfloat16 [1408], P('row'), may hold values from 0.25 to 1.75
- dec_qkv: bfloat16 [1408, 4224], P('row', 'col'), may hold values from -1 to 1
- dec_out: bfloat16 [1408, 1408], P('col', 'row'), may hold values from -0.15625 to 0.15625
- image_tokens: int32 [2, 8], P('grp'), may hold values from 1 to 32, 128 in all within a row
- text_gaps: int32 [2, 9], P('grp'), may hold values from 1 to 960, 1920 in all within a row
- doc_lengths: int32 [4], replicated, may hold values from 1 to 2048, 4096 in all
Outputs:
- hidden_out: bfloat16 [2, 2048, 1408], P('grp', 'col', 'row')
The draws below stay inside these ranges and needn't reach their ends.
All inputs are finite; a program needn't handle non-finite values.
Results may differ from the reference program's by a relative error of at most 0.0045.
The reference program's roundings to bfloat16 on the way count: a program that leaves them out, or rounds other values in their place, can miss the bound.
Values may be sent and summed in bfloat16 or wider, within the bound.
A program may use at most 64 MiB of HBM per device.

```python
import math
import jax
import jax.numpy as jnp
import numpy as np
from jax import lax

HEADS = 16
HEAD_DIM = 88
D = 1408
TPD = 256
IMGS = 8
SEGS = 4
HALVES = 2
PH = 512
MH = 128
SH = 2048


def paired_tokens(key, shape):
    base = jnp.clip(jax.random.normal(jax.random.fold_in(key, 1), shape, jnp.float32), -6.0, 6.0)
    return base.astype(jnp.bfloat16)


def drawn_projection(key):
    factor = D ** (-0.5)
    base = jnp.clip(jax.random.normal(jax.random.fold_in(key, 3), (D, HEADS, 3, HEAD_DIM), jnp.float32), -5.0, 5.0) * factor
    return base.reshape(D, 3 * D).astype(jnp.bfloat16)


def draw_patches(key, part):
    return paired_tokens(jax.random.fold_in(key, 41), (HALVES, PH, D))


def draw_text_embeds(key, part):
    return paired_tokens(jax.random.fold_in(key, 43), (HALVES, SH, D))


def draw_vis_qkv(key, part):
    return drawn_projection(jax.random.fold_in(key, 31))


def draw_dec_qkv(key, part):
    return drawn_projection(jax.random.fold_in(key, 37))


def shard_levels(own_key, dims, split, smallest, top_value):
    loudness = 1.0
    for axis_at, shards_of in split:
        steps = jax.random.uniform(jax.random.fold_in(jax.random.fold_in(own_key, 6), axis_at), (shards_of,), jnp.float32, smallest / len(split), top_value / len(split))
        loudness = loudness * jnp.repeat(jnp.exp(steps), dims[axis_at] // shards_of).reshape((-1,) + (1,) * (len(dims) - 1 - axis_at))
    return loudness


def profile(number_of, total, reach, lean):
    portions = [(1 << 20) // math.isqrt(rank ** lean) + 1 for rank in range(2, number_of + 1)]
    rest, holding = total - reach - (number_of - 1), [1] * (number_of - 1)
    while rest > 0:
        candidates = [i for i in range(number_of - 1) if holding[i] < reach]
        mass, remaining = sum([portions[i] for i in candidates]), rest
        for i in candidates:
            extra = min(reach - holding[i], max(1, remaining * portions[i] // mass), rest)
            holding[i] = holding[i] + extra
            rest = rest - extra
    return np.array([reach] + holding)


def ragged_sizes(rng, number_of, total, limit, lean):
    if number_of == 2:
        one = jax.random.randint(rng, (), max(1, total - limit), min(limit, total - 1) + 1)
        return jnp.stack([one, total - one])
    tallies = jnp.asarray(profile(number_of, total, limit, lean), jnp.int32)
    twos = (number_of - 1) // 2
    donor, receiver = tallies[1:1 + 2 * twos:2], tallies[2:2 + 2 * twos:2]
    room = jnp.minimum(donor - 1, limit - receiver)
    shifted = jax.random.randint(jax.random.fold_in(rng, 1), (twos,), 0, 1 << 20) % (room + 1)
    tallies = tallies.at[1:1 + 2 * twos:2].set(donor - shifted).at[2:2 + 2 * twos:2].set(receiver + shifted)
    return tallies[jax.random.permutation(jax.random.fold_in(rng, 2), number_of)]


def gaussian(stream_key, extent, deviation, bound, cuts=(), kind=jnp.bfloat16):
    values = jax.random.normal(stream_key, extent, jnp.float32) * deviation
    if len(cuts) > 0:
        values = shard_levels(stream_key, extent, cuts, -0.22, 0.18) * values
    return jnp.clip(values, min=-bound, max=bound).astype(kind)


def setup_inputs(seed: int = 0) -> dict:
    key_of = jax.random.split(jax.random.key(seed), 17)
    return {
        "patches": draw_patches(jax.random.fold_in(key_of[16], 71), 0),
        "vis_gain": jnp.clip(1.0 + 0.15 * jax.random.normal(key_of[1], (D,), jnp.float32), 0.25, 1.75).astype(jnp.bfloat16),
        "vis_bias": gaussian(key_of[2], (D,), 0.5, 3.0, ((0, 2),)),
        "vis_qkv": draw_vis_qkv(jax.random.fold_in(key_of[16], 71), 0),
        "vis_qkv_bias": gaussian(key_of[4], (3 * D,), 0.5, 3.0, ((0, 8),)),
        "vis_out": gaussian(key_of[5], (D, D), D ** -0.5, 0.15625, ((0, 8), (1, 2))),
        "vis_out_bias": gaussian(key_of[6], (D,), 0.5, 3.0, ((0, 2),)),
        "proj_weight": gaussian(key_of[7], (4, D, D), (4 * D) ** -0.5, 0.078125, ((1, 2), (2, 8))),
        "proj_bias": gaussian(key_of[8], (D,), 0.5, 3.0, ((0, 8),)),
        "text_embeds": draw_text_embeds(jax.random.fold_in(key_of[16], 71), 0),
        "dec_gain": jnp.clip(1.0 + 0.15 * jax.random.normal(key_of[10], (D,), jnp.float32), 0.25, 1.75).astype(jnp.bfloat16),
        "dec_qkv": draw_dec_qkv(jax.random.fold_in(key_of[16], 71), 0),
        "dec_out": gaussian(key_of[12], (D, D), D ** -0.5, 0.15625, ((0, 2), (1, 8))),
        "image_tokens": jax.vmap(lambda own: ragged_sizes(own, IMGS, MH, MH // 4, 2))(jax.random.split(key_of[13], HALVES)).reshape((HALVES, IMGS)).astype(jnp.int32),
        "text_gaps": jax.vmap(lambda own: ragged_sizes(own, IMGS + 1, SH - MH, (SH - MH) // 2, 2))(jax.random.split(key_of[14], HALVES)).reshape((HALVES, IMGS + 1)).astype(jnp.int32),
        "doc_lengths": ragged_sizes(key_of[15], SEGS, 2 * SH, SH, 1).astype(jnp.int32),
    }


def segment_of(index_values, lengths):
    ends = jnp.cumsum(lengths, dtype=jnp.int32)
    return lax.optimization_barrier(jnp.sum((index_values[:, None] >= ends[None, :]).astype(jnp.int32), axis=1, dtype=jnp.int32))

def insert_map(text_rows, image_lengths, gaps):
    offsets = jnp.cumsum(image_lengths, dtype=jnp.int32) - image_lengths
    starts = jnp.cumsum(gaps, dtype=jnp.int32)[:image_lengths.shape[0]] + offsets
    inside = (text_rows[:, None] >= starts[None, :]) & (text_rows[:, None] < (starts + image_lengths)[None, :])
    source = lax.optimization_barrier(jnp.sum(jnp.where(inside, offsets[None, :] + text_rows[:, None] - starts[None, :], 0), axis=1, dtype=jnp.int32))
    return (source.astype(jnp.int32), jnp.any(inside, axis=1))

def attend_heads(query, keys, values, allowed, scale):

    def one_head(parts):
        head_q, head_k, head_v = parts
        scores = jnp.dot(head_q, head_k.T, preferred_element_type=jnp.float32) * scale
        scores = jnp.where(allowed, scores, -1e+30)
        top = lax.optimization_barrier(jnp.max(scores, axis=1, keepdims=True))
        weights = jnp.where(allowed, jnp.exp(scores - top), 0.0)
        total = lax.optimization_barrier(jnp.sum(weights, axis=1, keepdims=True))
        mixed = jnp.dot(weights.astype(jnp.bfloat16), head_v, preferred_element_type=jnp.float32) / total
        return mixed.astype(jnp.bfloat16)
    return lax.map(one_head, (query, keys, values))

def split_heads(rows, count):
    shaped = rows.reshape(count, HEADS, 3, HEAD_DIM)
    return (jnp.transpose(shaped[:, :, 0], (1, 0, 2)), jnp.transpose(shaped[:, :, 1], (1, 0, 2)), jnp.transpose(shaped[:, :, 2], (1, 0, 2)))

def reference(patches, vis_gain, vis_bias, vis_qkv, vis_qkv_bias, vis_out, vis_out_bias, proj_weight, proj_bias, text_embeds, dec_gain, dec_qkv, dec_out, image_tokens, text_gaps, doc_lengths):
    width = HEADS * HEAD_DIM
    scale = HEAD_DIM ** (-0.5)
    pieces = []
    for half in range(HALVES):
        xfull = patches[half].astype(jnp.float32)
        mean = lax.optimization_barrier(jnp.sum(xfull, axis=1, keepdims=True)) / width
        variance = lax.optimization_barrier(jnp.sum(xfull * xfull, axis=1, keepdims=True)) / width - mean * mean
        normed = ((xfull - mean) * lax.rsqrt(variance + 1e-06) * vis_gain.astype(jnp.float32) + vis_bias.astype(jnp.float32)).astype(jnp.bfloat16)
        qkv_rows = (jnp.dot(normed, vis_qkv, preferred_element_type=jnp.float32) + vis_qkv_bias.astype(jnp.float32)).astype(jnp.bfloat16)
        query, keys, values = split_heads(qkv_rows, PH)
        image_id = segment_of(jnp.arange(PH, dtype=jnp.int32) // 4, image_tokens[half])
        allowed = image_id[:, None] == image_id[None, :]
        heads_out = attend_heads(query, keys, values, allowed, scale)
        attn = jnp.transpose(heads_out, (1, 0, 2)).reshape(PH, width)
        resid = (xfull + jnp.dot(attn, vis_out, preferred_element_type=jnp.float32) + vis_out_bias.astype(jnp.float32)).astype(jnp.bfloat16)
        merged = resid.reshape(MH, 4 * width)
        projected = jnp.dot(merged, proj_weight.reshape(4 * width, width), preferred_element_type=jnp.float32)
        source, is_image = insert_map(jnp.arange(SH, dtype=jnp.int32), image_tokens[half], text_gaps[half])
        placed = jnp.take(projected, source, axis=0) + proj_bias.astype(jnp.float32)
        pieces.append(jnp.where(is_image[:, None], placed, text_embeds[half].astype(jnp.float32)).astype(jnp.bfloat16))
    stacked = jnp.stack(pieces, axis=0)
    total_rows = HALVES * SH
    dec_input = jnp.transpose(stacked.reshape(HALVES, SH // TPD, TPD, width), (1, 0, 2, 3)).reshape(total_rows, width)
    xf = dec_input.astype(jnp.float32)
    mean_square = lax.optimization_barrier(jnp.sum(xf * xf, axis=1, keepdims=True)) / width
    normed = (xf * lax.rsqrt(mean_square + 1e-05) * dec_gain.astype(jnp.float32)).astype(jnp.bfloat16)
    qkv_rows = jnp.dot(normed, dec_qkv, preferred_element_type=jnp.float32).astype(jnp.bfloat16)
    query, keys, values = split_heads(qkv_rows, total_rows)
    positions = jnp.arange(total_rows, dtype=jnp.int32)
    doc = segment_of(positions, doc_lengths)
    allowed = (doc[:, None] == doc[None, :]) & (positions[None, :] <= positions[:, None])
    heads_out = attend_heads(query, keys, values, allowed, scale)
    attn = jnp.transpose(heads_out, (1, 0, 2)).reshape(total_rows, width)
    hidden = (xf + jnp.dot(attn, dec_out, preferred_element_type=jnp.float32)).astype(jnp.bfloat16)
    return jnp.transpose(hidden.reshape(SH // TPD, HALVES, TPD, width), (1, 0, 2, 3)).reshape(HALVES, SH, width)
```

```python
import functools

import jax
import jax.numpy as jnp
from jax import lax
from jax.experimental import pallas as pl
from jax.experimental.pallas import tpu as pltpu
from jax.sharding import PartitionSpec as P

HEADS = 16
HEAD_DIM = 88
PAD = 128
TPD = 256
LOG2E = 1.4426950408889634
F32 = jnp.float32
BF16 = jnp.bfloat16


def starts_of(index_values, lengths):
    ends = jnp.cumsum(lengths, dtype=jnp.int32)
    past = index_values[:, None] >= ends[None, :]
    return jnp.sum(jnp.where(past, lengths[None, :], 0), axis=1, dtype=jnp.int32)


def segment_of(index_values, lengths):
    ends = jnp.cumsum(lengths, dtype=jnp.int32)
    return jnp.sum((index_values[:, None] >= ends[None, :]).astype(jnp.int32), axis=1, dtype=jnp.int32)


def insert_map(text_rows, image_lengths, gaps):
    offsets = jnp.cumsum(image_lengths, dtype=jnp.int32) - image_lengths
    starts = jnp.cumsum(gaps, dtype=jnp.int32)[: image_lengths.shape[0]] + offsets
    inside = (text_rows[:, None] >= starts[None, :]) & (
        text_rows[:, None] < (starts + image_lengths)[None, :]
    )
    source = jnp.sum(
        jnp.where(inside, offsets[None, :] + text_rows[:, None] - starts[None, :], 0),
        axis=1,
        dtype=jnp.int32,
    )
    return (source, jnp.any(inside, axis=1))


def vis_head_kernel(
    x_ref, gain_ref, bias_ref, w_ref, wb_ref, ids_ref, idk_ref, o_ref, *, scale, width
):
    parts, count = x_ref.shape[0], x_ref.shape[1]
    one = jnp.zeros((count, 1), F32)
    two = jnp.zeros((count, 1), F32)
    for c in range(parts):
        x = x_ref[c].astype(F32)
        one += jnp.sum(x, axis=1, keepdims=True)
        two += jnp.sum(x * x, axis=1, keepdims=True)
    mean = one / width
    inv = lax.rsqrt(two / width - mean * mean + 1e-06)
    qkv = jnp.zeros((count, 3 * PAD), F32)
    for c in range(parts):
        x = x_ref[c].astype(F32)
        normed = ((x - mean) * inv * gain_ref[c].astype(F32) + bias_ref[c].astype(F32)).astype(BF16)
        qkv += jnp.dot(normed, w_ref[c], preferred_element_type=F32)
    qkv = (qkv + wb_ref[...].astype(F32)).astype(BF16)
    q, k, v = qkv[:, :PAD], qkv[:, PAD : 2 * PAD], qkv[:, 2 * PAD :]
    scores = lax.dot_general(q, k, (((1,), (1,)), ((), ())), preferred_element_type=F32)
    scores = scores * (scale * LOG2E)
    allowed = ids_ref[...] == idk_ref[...]
    scores = jnp.where(allowed, scores, -1e30)
    top = jnp.max(scores, axis=1, keepdims=True)
    weights = jnp.where(allowed, jnp.exp2(scores - top), 0.0)
    total = jnp.sum(weights, axis=1, keepdims=True)
    mixed = jnp.dot(weights.astype(BF16), v, preferred_element_type=F32) / total
    o_ref[...] = mixed.astype(BF16)


def vis_head(x, gain, bias, w, wb, ids, scale):
    count = x.shape[1]
    return pl.pallas_call(
        functools.partial(vis_head_kernel, scale=scale, width=HEADS * HEAD_DIM),
        out_shape=jax.ShapeDtypeStruct((count, PAD), BF16),
        compiler_params=pltpu.CompilerParams(vmem_limit_bytes=48 << 20),
        name="vis_head",
    )(x, gain, bias, w, wb, ids[:, None], ids[None, :])


def dec_qkv_kernel(x_ref, gain_ref, w_ref, o_ref, *, width):
    parts, count = x_ref.shape[1], x_ref.shape[2]
    squares = jnp.zeros((count, 1), F32)
    for r in range(parts):
        x = x_ref[0, r].astype(F32)
        squares += jnp.sum(x * x, axis=1, keepdims=True)
    inv = lax.rsqrt(squares / width + 1e-05)
    qkv = jnp.zeros((count, 3 * PAD), F32)
    for r in range(parts):
        x = x_ref[0, r].astype(F32)
        normed = (x * inv * gain_ref[r].astype(F32)).astype(BF16)
        qkv += jnp.dot(normed, w_ref[r], preferred_element_type=F32)
    o_ref[0] = qkv.astype(BF16)


def dec_rows(x, gain, w, tile):
    groups, parts, count, depth = x.shape
    return pl.pallas_call(
        functools.partial(dec_qkv_kernel, width=HEADS * HEAD_DIM),
        grid=(groups, count // tile),
        in_specs=[
            pl.BlockSpec((1, parts, tile, depth), lambda i, j: (i, 0, j, 0)),
            pl.BlockSpec(gain.shape, lambda i, j: (0, 0, 0)),
            pl.BlockSpec(w.shape, lambda i, j: (0, 0, 0)),
        ],
        out_specs=pl.BlockSpec((1, tile, 3 * PAD), lambda i, j: (i, j, 0)),
        out_shape=jax.ShapeDtypeStruct((groups, count, 3 * PAD), BF16),
        compiler_params=pltpu.CompilerParams(vmem_limit_bytes=48 << 20),
        name="dec_rows",
    )(x, gain, w)


def dec_attn_kernel(low_ref, q_ref, start_ref, pos_ref, k_ref, v_ref, o_ref, *, scale):
    b = pl.program_id(0)
    q = q_ref[...]
    begin = start_ref[...]
    at = pos_ref[...]
    count = q.shape[0]
    chunk = 2 * TPD

    def step(j, carry):
        best, norm, accum = carry
        rows = pl.ds(pl.multiple_of(j * TPD, TPD), TPD)
        k = jnp.concatenate([k_ref[0, rows], k_ref[1, rows]], axis=0)
        v = jnp.concatenate([v_ref[0, rows], v_ref[1, rows]], axis=0)
        scores = lax.dot_general(q, k, (((1,), (1,)), ((), ())), preferred_element_type=F32)
        scores = scores * (scale * LOG2E)
        key_at = j * chunk + lax.broadcasted_iota(jnp.int32, (count, chunk), 1)
        allowed = (key_at >= begin) & (key_at <= at)
        scores = jnp.where(allowed, scores, -1e30)
        new_best = jnp.maximum(best, jnp.max(scores, axis=1, keepdims=True))
        weights = jnp.where(allowed, jnp.exp2(scores - new_best), 0.0)
        factor = jnp.exp2(best - new_best)
        norm = norm * factor + jnp.sum(weights, axis=1, keepdims=True)
        accum = accum * factor + jnp.dot(weights.astype(BF16), v, preferred_element_type=F32)
        return new_best, norm, accum

    init = (
        jnp.full((count, 1), -1e30, F32),
        jnp.zeros((count, 1), F32),
        jnp.zeros((count, PAD), F32),
    )
    best, norm, accum = lax.fori_loop(low_ref[b], b + 1, step, init)
    o_ref[...] = (accum / norm).astype(BF16)


def dec_attn(q, k, v, begin, at, scale):
    count = q.shape[0]
    low = begin[::TPD] // (2 * TPD)
    return pl.pallas_call(
        functools.partial(dec_attn_kernel, scale=scale),
        grid_spec=pltpu.PrefetchScalarGridSpec(
            num_scalar_prefetch=1,
            grid=(count // TPD,),
            in_specs=[
                pl.BlockSpec((TPD, PAD), lambda i, s: (i, 0)),
                pl.BlockSpec((TPD, 1), lambda i, s: (i, 0)),
                pl.BlockSpec((TPD, 1), lambda i, s: (i, 0)),
                pl.BlockSpec(k.shape, lambda i, s: (0, 0, 0)),
                pl.BlockSpec(v.shape, lambda i, s: (0, 0, 0)),
            ],
            out_specs=pl.BlockSpec((TPD, PAD), lambda i, s: (i, 0)),
        ),
        out_shape=jax.ShapeDtypeStruct((count, PAD), BF16),
        compiler_params=pltpu.CompilerParams(vmem_limit_bytes=48 << 20),
        name="dec_attn",
    )(low, q, begin[:, None], at[:, None], k, v)


def pad_parts(w):
    lead = w.shape[:-1]
    w = w.reshape(lead + (3, HEAD_DIM))
    w = jnp.pad(w, [(0, 0)] * (len(lead) + 1) + [(0, PAD - HEAD_DIM)])
    return w.reshape(lead + (3 * PAD,))


def per_device(
    patches,
    vis_gain,
    vis_bias,
    vis_qkv,
    vis_qkv_bias,
    vis_out,
    vis_out_bias,
    proj_weight,
    proj_bias,
    text_embeds,
    dec_gain,
    dec_qkv,
    dec_out,
    image_tokens,
    text_gaps,
    doc_lengths,
):
    scale = HEAD_DIM ** (-0.5)
    C = lax.axis_size("col")
    R = lax.axis_size("row")
    c = lax.axis_index("col")
    r = lax.axis_index("row")
    g = lax.axis_index("grp")
    hr = HEADS // R
    hc = HEADS // C
    share = R // hc
    image_lengths = image_tokens[0]
    gaps = text_gaps[0]
    text = text_embeds[0]
    half_rows = text.shape[0] * C
    own_text = text.shape[0]

    x_all = lax.all_gather(patches[0], ("col", "row"), axis=0)
    x_all = x_all.reshape(C, R * patches.shape[1], patches.shape[2])
    patch_total = x_all.shape[1]
    head_of = c * hr // C
    small = lax.all_gather(jnp.stack([vis_gain, vis_bias]), "col", axis=0)
    wv = lax.all_gather(vis_qkv, "col", axis=0)
    wv = lax.dynamic_slice_in_dim(wv, head_of * 3 * HEAD_DIM, 3 * HEAD_DIM, axis=2)
    wv = pad_parts(wv)
    wvb = pad_parts(lax.dynamic_slice_in_dim(vis_qkv_bias, head_of * 3 * HEAD_DIM, 3 * HEAD_DIM, 0))
    text_all = lax.all_gather(text, ("col", "row"), axis=0).reshape(C, R, own_text, text.shape[1])
    vis_out_all = lax.all_gather(vis_out, "row", axis=0, tiled=True)
    wd = jnp.transpose(dec_qkv.reshape(dec_qkv.shape[0], hc, 3 * HEAD_DIM), (1, 0, 2))
    wd = pad_parts(jnp.repeat(wd, share, axis=0) if share > 1 else wd)
    wd = lax.all_to_all(wd, "row", 0, 0)
    dec_out_all = lax.all_gather(dec_out, ("col", "row"), axis=0)
    dec_out_all = dec_out_all.reshape(C, R, hc, HEAD_DIM, dec_out.shape[1])
    gain_all = lax.all_gather(dec_gain, "row", axis=0)[:, None]

    patch_ids = segment_of(jnp.arange(patch_total, dtype=jnp.int32) // 4, image_lengths)
    attn = vis_head(x_all, small[:, :1], small[:, 1:], wv, wvb[None], patch_ids, scale)
    attn_all = lax.all_gather(attn[:, :HEAD_DIM], ("row", "col"), axis=0)
    attn_all = attn_all.reshape(R, C, patch_total, HEAD_DIM)[:, :: C // hr]
    attn_all = jnp.transpose(attn_all, (2, 0, 1, 3)).reshape(patch_total, HEADS * HEAD_DIM)
    own_x = lax.dynamic_index_in_dim(x_all, c, 0, keepdims=False)
    resid = (
        own_x.astype(F32)
        + jnp.dot(attn_all, vis_out_all, preferred_element_type=F32)
        + vis_out_bias.astype(F32)
    ).astype(BF16)
    merged = resid.reshape(patch_total // 4, 4 * resid.shape[1])
    partial = jnp.dot(
        merged, proj_weight.reshape(4 * proj_weight.shape[1], -1), preferred_element_type=F32
    )
    image_rows = (lax.psum(partial, "col") + proj_bias.astype(F32)).astype(BF16)
    image_all = lax.all_gather(image_rows, "row", axis=0)

    text_qkv = dec_rows(text_all, gain_all, wd, TPD).reshape(half_rows, 3 * PAD)
    image_qkv = dec_rows(image_all[None], gain_all, wd, image_rows.shape[0])[0]
    source, inside = insert_map(jnp.arange(half_rows, dtype=jnp.int32), image_lengths, gaps)
    pick = jnp.where(inside, source, -1)
    hot = (pick[:, None] == jnp.arange(image_rows.shape[0], dtype=jnp.int32)[None]).astype(BF16)
    placed = jnp.dot(hot, image_qkv, preferred_element_type=F32).astype(BF16)
    qkv = jnp.where(inside[:, None], placed, text_qkv)
    both = lax.all_gather(qkv[:, PAD:], "grp", axis=0)
    t = jnp.arange(half_rows, dtype=jnp.int32)
    at = t // TPD * (2 * TPD) + g * TPD + t % TPD
    begin = starts_of(at, doc_lengths)
    out = dec_attn(qkv[:, :PAD], both[..., :PAD], both[..., PAD:], begin, at, scale)

    mine = half_rows // (C * R)
    spread = out[:, :HEAD_DIM].reshape(C * R, mine, HEAD_DIM)
    rows = lax.all_to_all(spread, ("col", "row"), 0, 0)
    rows = rows.reshape(C, R, mine, HEAD_DIM)[:, ::share]
    delta = jnp.einsum(
        "chte,crhef->rtf", rows, dec_out_all, preferred_element_type=F32
    ).astype(BF16)
    delta = lax.all_to_all(delta, "row", 0, 0).reshape(own_text, text.shape[1])
    own_hot = lax.dynamic_slice_in_dim(hot, c * own_text, own_text, 0)
    own_inside = lax.dynamic_slice_in_dim(inside, c * own_text, own_text, 0)
    own_placed = jnp.dot(own_hot, image_rows, preferred_element_type=F32)
    dec_input = jnp.where(own_inside[:, None], own_placed, text.astype(F32))
    return (dec_input + delta.astype(F32)).astype(BF16)[None]


def solution(mesh):
    return jax.shard_map(
        per_device,
        mesh=mesh,
        in_specs=(
            P("grp", "row", "col"),
            P("col"),
            P("col"),
            P("col", "row"),
            P("row"),
            P("row", "col"),
            P("col"),
            P(None, "col", "row"),
            P("row"),
            P("grp", "col", "row"),
            P("row"),
            P("row", "col"),
            P("col", "row"),
            P("grp", None),
            P("grp", None),
            P(),
        ),
        out_specs=P("grp", "col", "row"),
        check_vma=False,
    )
```

```python
import functools

import jax
import jax.numpy as jnp
from jax import lax
from jax.experimental import pallas as pl
from jax.experimental.pallas import tpu as pltpu
from jax.sharding import PartitionSpec as P

HEADS = 16
HEAD_DIM = 88
PAD = 128
TPD = 256
LOG2E = 1.4426950408889634
F32 = jnp.float32
BF16 = jnp.bfloat16


def starts_of(index_values, lengths):
    ends = jnp.cumsum(lengths, dtype=jnp.int32)
    past = index_values[:, None] >= ends[None, :]
    return jnp.sum(jnp.where(past, lengths[None, :], 0), axis=1, dtype=jnp.int32)


def segment_of(index_values, lengths):
    ends = jnp.cumsum(lengths, dtype=jnp.int32)
    return jnp.sum((index_values[:, None] >= ends[None, :]).astype(jnp.int32), axis=1, dtype=jnp.int32)


def insert_map(text_rows, image_lengths, gaps):
    offsets = jnp.cumsum(image_lengths, dtype=jnp.int32) - image_lengths
    starts = jnp.cumsum(gaps, dtype=jnp.int32)[: image_lengths.shape[0]] + offsets
    inside = (text_rows[:, None] >= starts[None, :]) & (
        text_rows[:, None] < (starts + image_lengths)[None, :]
    )
    source = jnp.sum(
        jnp.where(inside, offsets[None, :] + text_rows[:, None] - starts[None, :], 0),
        axis=1,
        dtype=jnp.int32,
    )
    return (source, jnp.any(inside, axis=1))


class Links:
    def __init__(self, send, recv, rows, cols):
        self.send, self.recv = send, recv
        self.rows, self.cols = rows, cols
        self.r, self.c = lax.axis_index("row"), lax.axis_index("col")
        self.g = lax.axis_index("grp")
        self.high, self.low = self.r // 2, self.r % 2
        self.count = 0
        self.taken = 0
        self.pending = []

    def slots(self, number):
        base = self.taken
        self.taken += number
        return base

    def push(self, src, dst, slot, **where):
        copy = pltpu.make_async_remote_copy(
            src_ref=src,
            dst_ref=dst,
            send_sem=self.send.at[self.count],
            recv_sem=self.recv.at[slot],
            device_id=where,
            device_id_type=pl.DeviceIdType.MESH,
        )
        self.count += 1
        copy.start()
        self.pending.append(copy)

    def arrived(self, dst, slot):
        pltpu.make_async_remote_copy(
            src_ref=dst,
            dst_ref=dst,
            send_sem=self.send.at[0],
            recv_sem=self.recv.at[slot],
            device_id={"row": self.r},
            device_id_type=pl.DeviceIdType.MESH,
        ).wait_recv()

    def row_peer(self, step):
        return (self.high + step) % (self.rows // 2) * 2 + self.low

    def row_start(self, src, dst, base):
        other = self.high * 2 + 1 - self.low
        for step in range(1, self.rows // 2):
            self.push(src, dst.at[self.r], base + self.r, row=self.row_peer(step))
        self.push(src, dst.at[self.r], base + self.r, row=other)

    def row_forward(self, dst, base):
        other = self.high * 2 + 1 - self.low
        for step in range(1, self.rows // 2):
            at = self.row_peer(self.rows // 2 - step)
            self.arrived(dst.at[at], base + at)
            self.push(dst.at[at], dst.at[at], base + at, row=other)

    def row_finish(self, dst, base):
        for step in range(self.rows // 2):
            at = (self.high + step) % (self.rows // 2) * 2 + 1 - self.low
            self.arrived(dst.at[at], base + at)

    def col_start(self, src, dst, base):
        for step in range(1, self.cols):
            self.push(src, dst, base + self.c, col=(self.c + step) % self.cols)

    def col_finish(self, dst, base):
        for step in range(1, self.cols):
            at = (self.c + step) % self.cols
            self.arrived(dst.at[at], base + at)


def front_kernel(
    patch_ref, small_ref, wv_in, wvb_ref, ids_ref, idk_ref, vo_in, vob_ref, proj_ref, projb_ref,
    text_in, gain_in, wd_in, meta_in,
    qkv_ref, img_ref, image_ref, meta_ref,
    x_ref, s_ref, wv_ref, vo_ref, wd_ref, gain_ref, text_ref, at_ref, part_ref,
    send, recv, local,
    *, rows, cols, hr, scale, width,
):
    net = Links(send, recv, rows, cols)
    r, c, g = net.r, net.c, net.g
    barrier = pltpu.get_barrier_semaphore()
    for step in range(1, rows):
        pl.semaphore_signal(barrier, inc=1, device_id={"row": (r + step) % rows},
                            device_id_type=pl.DeviceIdType.MESH)
    for step in range(1, cols):
        pl.semaphore_signal(barrier, inc=1, device_id={"col": (c + step) % cols},
                            device_id_type=pl.DeviceIdType.MESH)
    pl.semaphore_signal(barrier, inc=1, device_id={"grp": 1 - g},
                        device_id_type=pl.DeviceIdType.MESH)
    pl.semaphore_wait(barrier, rows + cols - 1)

    own = [
        (patch_ref, x_ref.at[c, r]),
        (small_ref, s_ref.at[c]),
        (wv_in.at[c * hr // cols], wv_ref.at[c]),
        (vo_in, vo_ref.at[r]),
        (wd_in.at[r], wd_ref.at[r]),
        (gain_in, gain_ref.at[r]),
        (text_in, text_ref.at[c, r]),
        (meta_in, meta_ref.at[g]),
    ]
    own = [pltpu.make_async_copy(a, b, local.at[i]) for i, (a, b) in enumerate(own)]
    for copy in own:
        copy.start()

    x_row, x_col = net.slots(rows), net.slots(cols)
    s_col, wv_col = net.slots(cols), net.slots(cols)
    vo_row, wd_row, gain_row = net.slots(rows), net.slots(rows), net.slots(rows)
    text_row, text_col = net.slots(rows), net.slots(cols)
    at_row, at_col = net.slots(rows), net.slots(cols)
    part_col, img_row, meta_grp = net.slots(cols), net.slots(rows), net.slots(1)
    kv_grp, imgkv_grp = net.slots(1), net.slots(1)

    net.row_start(patch_ref, x_ref.at[c], x_row)
    net.col_start(small_ref, s_ref.at[c], s_col)
    for step in range(1, cols):
        to = (c + step) % cols
        net.push(wv_in.at[to * hr // cols], wv_ref.at[c], wv_col + c, col=to)
    net.push(meta_in, meta_ref.at[g], meta_grp, grp=1 - g)
    net.row_start(gain_in, gain_ref, gain_row)
    net.row_start(text_in, text_ref.at[c], text_row)
    net.row_start(vo_in, vo_ref, vo_row)
    for step in range(1, rows):
        to = (r + step) % rows
        net.push(wd_in.at[to], wd_ref.at[r], wd_row + r, row=to)
    for copy in own:
        copy.wait()
    net.row_forward(x_ref.at[c], x_row)
    net.row_finish(x_ref.at[c], x_row)
    net.col_start(x_ref.at[c], x_ref.at[c], x_col)
    net.col_finish(s_ref, s_col)
    net.col_finish(wv_ref, wv_col)
    net.col_finish(x_ref, x_col)

    count = rows * patch_ref.shape[0]
    depth = patch_ref.shape[1]
    one = jnp.zeros((count, 1), F32)
    two = jnp.zeros((count, 1), F32)
    for i in range(cols):
        x = x_ref[i].reshape(count, depth).astype(F32)
        one += jnp.sum(x, axis=1, keepdims=True)
        two += jnp.sum(x * x, axis=1, keepdims=True)
    mean = one / width
    inv = lax.rsqrt(two / width - mean * mean + 1e-06)
    qkv = jnp.zeros((count, 3 * PAD), F32)
    for i in range(cols):
        x = x_ref[i].reshape(count, depth).astype(F32)
        normed = ((x - mean) * inv * s_ref[i, 0:1] + s_ref[i, 1:2]).astype(BF16)
        qkv += jnp.dot(normed, wv_ref[i], preferred_element_type=F32)
    qkv = (qkv + wvb_ref[...].astype(F32)).astype(BF16)
    q, k, v = qkv[:, :PAD], qkv[:, PAD : 2 * PAD], qkv[:, 2 * PAD :]
    scores = lax.dot_general(q, k, (((1,), (1,)), ((), ())), preferred_element_type=F32)
    scores = scores * (scale * LOG2E)
    allowed = ids_ref[...] == idk_ref[...]
    scores = jnp.where(allowed, scores, -1e30)
    top = jnp.max(scores, axis=1, keepdims=True)
    weights = jnp.where(allowed, jnp.exp2(scores - top), 0.0)
    total = jnp.sum(weights, axis=1, keepdims=True)
    mixed = jnp.dot(weights.astype(BF16), v, preferred_element_type=F32) / total
    mine = c * hr // cols
    at_ref[mine, r] = mixed.astype(BF16)
    net.row_start(at_ref.at[mine, r], at_ref.at[mine], at_row)
    net.row_forward(at_ref.at[mine], at_row)
    net.row_forward(text_ref.at[c], text_row)
    net.row_finish(at_ref.at[mine], at_row)
    for step in range(1, hr):
        to = (c + step * (cols // hr)) % cols
        net.push(at_ref.at[mine], at_ref.at[mine], at_col + mine, col=to)
    net.row_forward(vo_ref, vo_row)
    net.row_finish(vo_ref, vo_row)
    for step in range(1, hr):
        other = (mine + step) % hr
        net.arrived(at_ref.at[other], at_col + other)

    delta = x_ref[c].reshape(count, depth).astype(F32) + vob_ref[...].astype(F32)
    for i in range(rows):
        for h in range(hr):
            delta += jnp.dot(at_ref[h, i], vo_ref[i, h], preferred_element_type=F32)
    tokens = count // 4
    resid = delta.astype(BF16).reshape(rows, 4, tokens // rows, depth)
    partial = jnp.zeros(part_ref.shape[1:], F32)
    for i in range(4):
        quarter = resid[:, i].reshape(tokens, depth)
        partial += jnp.dot(quarter, proj_ref[i], preferred_element_type=F32)
    part_ref[c] = partial
    net.col_start(part_ref.at[c], part_ref.at[c], part_col)
    net.col_finish(part_ref, part_col)
    image = projb_ref[...].astype(F32)
    for i in range(cols):
        image = image + part_ref[i]
    image_ref[r] = image.astype(BF16)
    net.row_start(image_ref.at[r], image_ref, img_row)
    net.row_forward(gain_ref, gain_row)
    net.row_finish(gain_ref, gain_row)
    net.row_finish(text_ref.at[c], text_row)
    net.col_start(text_ref.at[c], text_ref.at[c], text_col)
    for step in range(1, rows):
        at = (r + step) % rows
        net.arrived(wd_ref.at[at], wd_row + at)
    net.row_forward(image_ref, img_row)

    def head_rows(part):
        number = part(0).shape[0]
        squares = jnp.zeros((number, 1), F32)
        for i in range(rows):
            x = part(i).astype(F32)
            squares += jnp.sum(x * x, axis=1, keepdims=True)
        inv = lax.rsqrt(squares / width + 1e-05)
        total = jnp.zeros((number, 3 * PAD), F32)
        for i in range(rows):
            normed = (part(i).astype(F32) * inv * gain_ref[i, 0:1]).astype(BF16)
            total += jnp.dot(normed, wd_ref[i], preferred_element_type=F32)
        return total.astype(BF16)

    own_rows = text_in.shape[0]

    def text_block(at):
        @pl.loop(0, own_rows // TPD)
        def _(j):
            start = pl.multiple_of(j * TPD, TPD)
            found = head_rows(lambda i: text_ref[at, i, pl.ds(start, TPD)])
            qkv_ref[g, pl.ds(pl.multiple_of(at * own_rows + start, TPD), TPD)] = found

    text_block(c)
    net.row_finish(image_ref, img_row)
    img_ref[g] = head_rows(lambda i: image_ref[i])
    net.push(img_ref.at[g], img_ref.at[g], imgkv_grp, grp=1 - g)
    net.col_finish(text_ref, text_col)
    for step in range(1, cols):
        text_block((c + step) % cols)
    net.push(qkv_ref.at[g], qkv_ref.at[g], kv_grp, grp=1 - g)
    net.arrived(meta_ref.at[1 - g], meta_grp)
    net.arrived(img_ref.at[1 - g], imgkv_grp)
    net.arrived(qkv_ref.at[1 - g], kv_grp)
    for copy in net.pending:
        copy.wait_send()


def front(patch, small, wv, wvb, ids, vo, vob, proj, projb, text, gain, wd, meta, rows, cols, scale):
    hr = wv.shape[0]
    count = rows * patch.shape[0]
    half = cols * text.shape[0]
    tokens = count // 4
    depth = proj.shape[2]
    args = (patch, small, wv, wvb, ids[:, None], ids[None, :], vo, vob, proj, projb, text, gain, wd, meta)
    sends = 6 * (rows - 1) + (rows - 1) + 6 * (cols - 1) + 3
    slots = 7 * rows + 6 * cols + 3
    vmem = pl.BlockSpec(memory_space=pltpu.VMEM)
    return pl.pallas_call(
        functools.partial(
            front_kernel, rows=rows, cols=cols, hr=hr, scale=scale, width=HEADS * HEAD_DIM
        ),
        in_specs=[vmem] * len(args),
        out_specs=[vmem] * 4,
        out_shape=[
            jax.ShapeDtypeStruct((2, half, 3 * PAD), BF16),
            jax.ShapeDtypeStruct((2, tokens, 3 * PAD), BF16),
            jax.ShapeDtypeStruct((rows, tokens, depth), BF16),
            jax.ShapeDtypeStruct((2,) + meta.shape, jnp.int32),
        ],
        scratch_shapes=[
            pltpu.VMEM((cols, rows) + patch.shape, BF16),
            pltpu.VMEM((cols,) + small.shape, F32),
            pltpu.VMEM((cols,) + wv.shape[1:], BF16),
            pltpu.VMEM((rows,) + vo.shape, BF16),
            pltpu.VMEM(wd.shape, BF16),
            pltpu.VMEM((rows,) + gain.shape, F32),
            pltpu.VMEM((cols, rows) + text.shape, BF16),
            pltpu.VMEM((hr, rows, count, PAD), BF16),
            pltpu.VMEM((cols, tokens, depth), F32),
            pltpu.SemaphoreType.DMA((sends,)),
            pltpu.SemaphoreType.DMA((slots,)),
            pltpu.SemaphoreType.DMA((8,)),
        ],
        compiler_params=pltpu.CompilerParams(
            collective_id=0, has_side_effects=True, vmem_limit_bytes=56 << 20
        ),
        name="front",
    )(*args)


def dec_attn_kernel(low_ref, q_ref, start_ref, pos_ref, k_ref, v_ref, o_ref, *, scale):
    b = pl.program_id(0)
    q = q_ref[...]
    begin = start_ref[...]
    at = pos_ref[...]
    count = q.shape[0]
    chunk = 2 * TPD

    def step(j, carry):
        best, norm, accum = carry
        rows = pl.ds(pl.multiple_of(j * TPD, TPD), TPD)
        k = jnp.concatenate([k_ref[0, rows], k_ref[1, rows]], axis=0)
        v = jnp.concatenate([v_ref[0, rows], v_ref[1, rows]], axis=0)
        scores = lax.dot_general(q, k, (((1,), (1,)), ((), ())), preferred_element_type=F32)
        scores = scores * (scale * LOG2E)
        key_at = j * chunk + lax.broadcasted_iota(jnp.int32, (count, chunk), 1)
        allowed = (key_at >= begin) & (key_at <= at)
        scores = jnp.where(allowed, scores, -1e30)
        new_best = jnp.maximum(best, jnp.max(scores, axis=1, keepdims=True))
        weights = jnp.where(allowed, jnp.exp2(scores - new_best), 0.0)
        factor = jnp.exp2(best - new_best)
        norm = norm * factor + jnp.sum(weights, axis=1, keepdims=True)
        accum = accum * factor + jnp.dot(weights.astype(BF16), v, preferred_element_type=F32)
        return new_best, norm, accum

    init = (
        jnp.full((count, 1), -1e30, F32),
        jnp.zeros((count, 1), F32),
        jnp.zeros((count, PAD), F32),
    )
    best, norm, accum = lax.fori_loop(low_ref[b], b + 1, step, init)
    o_ref[...] = (accum / norm).astype(BF16)


def dec_attn(q, k, v, begin, at, scale):
    count = q.shape[0]
    low = begin[::TPD] // (2 * TPD)
    return pl.pallas_call(
        functools.partial(dec_attn_kernel, scale=scale),
        grid_spec=pltpu.PrefetchScalarGridSpec(
            num_scalar_prefetch=1,
            grid=(count // TPD,),
            in_specs=[
                pl.BlockSpec((TPD, PAD), lambda i, s: (i, 0)),
                pl.BlockSpec((TPD, 1), lambda i, s: (i, 0)),
                pl.BlockSpec((TPD, 1), lambda i, s: (i, 0)),
                pl.BlockSpec(k.shape, lambda i, s: (0, 0, 0)),
                pl.BlockSpec(v.shape, lambda i, s: (0, 0, 0)),
            ],
            out_specs=pl.BlockSpec((TPD, PAD), lambda i, s: (i, 0)),
        ),
        out_shape=jax.ShapeDtypeStruct((count, PAD), BF16),
        compiler_params=pltpu.CompilerParams(vmem_limit_bytes=48 << 20),
        name="dec_attn",
    )(low, q, begin[:, None], at[:, None], k, v)


def pad_parts(w):
    lead = w.shape[:-1]
    w = w.reshape(lead + (3, HEAD_DIM))
    w = jnp.pad(w, [(0, 0)] * (len(lead) + 1) + [(0, PAD - HEAD_DIM)])
    return w.reshape(lead + (3 * PAD,))


def per_device(
    patches,
    vis_gain,
    vis_bias,
    vis_qkv,
    vis_qkv_bias,
    vis_out,
    vis_out_bias,
    proj_weight,
    proj_bias,
    text_embeds,
    dec_gain,
    dec_qkv,
    dec_out,
    image_tokens,
    text_gaps,
    doc_lengths,
):
    scale = HEAD_DIM ** (-0.5)
    C = lax.axis_size("col")
    R = lax.axis_size("row")
    c = lax.axis_index("col")
    r = lax.axis_index("row")
    g = lax.axis_index("grp")
    hr = HEADS // R
    hc = HEADS // C
    share = R // hc
    image_lengths = image_tokens[0]
    gaps = text_gaps[0]
    text = text_embeds[0]
    half_rows = text.shape[0] * C
    own_text = text.shape[0]

    dec_out_all = lax.all_gather(dec_out, ("col", "row"), axis=0)
    dec_out_all = dec_out_all.reshape(C, R, hc, HEAD_DIM, dec_out.shape[1])
    patch_total = R * patches.shape[1]
    head_of = c * hr // C
    small = jnp.pad(jnp.stack([vis_gain, vis_bias]).astype(F32), ((0, 6), (0, 0)))
    wv = pad_parts(jnp.transpose(vis_qkv.reshape(-1, hr, 3 * HEAD_DIM), (1, 0, 2)))
    wvb = lax.dynamic_slice_in_dim(vis_qkv_bias, head_of * 3 * HEAD_DIM, 3 * HEAD_DIM, 0)
    wvb = pad_parts(wvb)[None]
    vo = jnp.pad(vis_out.reshape(hr, HEAD_DIM, -1), ((0, 0), (0, PAD - HEAD_DIM), (0, 0)))
    wd = jnp.transpose(dec_qkv.reshape(dec_qkv.shape[0], hc, 3 * HEAD_DIM), (1, 0, 2))
    wd = pad_parts(jnp.repeat(wd, share, axis=0) if share > 1 else wd)
    gain = jnp.pad(dec_gain.astype(F32)[None], ((0, 7), (0, 0)))
    images = image_tokens.shape[1]
    meta = jnp.concatenate([image_lengths, gaps])
    meta = jnp.pad(meta[None], ((0, 7), (0, PAD - meta.shape[0])))
    patch = patches[0].reshape(-1, 4, patches.shape[2])
    patch = jnp.transpose(patch, (1, 0, 2)).reshape(patches.shape[1:])
    patch_ids = segment_of(jnp.arange(patch_total // 4, dtype=jnp.int32), image_lengths)
    patch_ids = jnp.tile(patch_ids.reshape(R, 1, -1), (1, 4, 1)).reshape(patch_total)
    qkv_text, qkv_image, image_all, meta = front(
        patch, small, wv, wvb, patch_ids, vo, vis_out_bias[None], proj_weight,
        proj_bias[None], text, gain, wd, meta, R, C, scale,
    )
    image_rows = lax.dynamic_index_in_dim(image_all, r, 0, keepdims=False)

    t = jnp.arange(half_rows, dtype=jnp.int32)

    def hot_of(lengths, spaces):
        source, inside = insert_map(t, lengths, spaces)
        pick = jnp.where(inside, source, -1)
        hot = pick[:, None] == jnp.arange(image_rows.shape[0], dtype=jnp.int32)[None]
        return hot.astype(BF16), inside

    hot, inside = hot_of(image_lengths, gaps)
    merged = []
    for half in range(2):
        hot_half, inside_half = hot_of(
            meta[half, 0, :images], meta[half, 0, images : 2 * images + 1]
        )
        placed = jnp.dot(hot_half, qkv_image[half], preferred_element_type=F32).astype(BF16)
        merged.append(jnp.where(inside_half[:, None], placed, qkv_text[half]))
    both = jnp.stack(merged)
    query = lax.dynamic_index_in_dim(both, g, 0, keepdims=False)[:, :PAD]
    at = t // TPD * (2 * TPD) + g * TPD + t % TPD
    begin = starts_of(at, doc_lengths)
    out = dec_attn(query, both[..., PAD : 2 * PAD], both[..., 2 * PAD :], begin, at, scale)

    mine = half_rows // (C * R)
    spread = out[:, :HEAD_DIM].reshape(C * R, mine, HEAD_DIM)
    rows = lax.all_to_all(spread, ("col", "row"), 0, 0)
    rows = rows.reshape(C, R, mine, HEAD_DIM)[:, ::share]
    delta = jnp.einsum(
        "chte,crhef->rtf", rows, dec_out_all, preferred_element_type=F32
    ).astype(BF16)
    delta = lax.all_to_all(delta, "row", 0, 0).reshape(own_text, text.shape[1])
    own_hot = lax.dynamic_slice_in_dim(hot, c * own_text, own_text, 0)
    own_inside = lax.dynamic_slice_in_dim(inside, c * own_text, own_text, 0)
    own_placed = jnp.dot(own_hot, image_rows, preferred_element_type=F32)
    dec_input = jnp.where(own_inside[:, None], own_placed, text.astype(F32))
    return (dec_input + delta.astype(F32)).astype(BF16)[None]


def solution(mesh):
    return jax.shard_map(
        per_device,
        mesh=mesh,
        in_specs=(
            P("grp", "row", "col"),
            P("col"),
            P("col"),
            P("col", "row"),
            P("row"),
            P("row", "col"),
            P("col"),
            P(None, "col", "row"),
            P("row"),
            P("grp", "col", "row"),
            P("row"),
            P("row", "col"),
            P("col", "row"),
            P("grp", None),
            P("grp", None),
            P(),
        ),
        out_specs=P("grp", "col", "row"),
        check_vma=False,
    )
```

```python
import functools

import jax
import jax.numpy as jnp
from jax import lax
from jax.experimental import pallas as pl
from jax.experimental.pallas import tpu as pltpu
from jax.sharding import PartitionSpec as P

HEADS = 16
HEAD_DIM = 88
PAD = 128
TPD = 256
LOG2E = 1.4426950408889634
F32 = jnp.float32
BF16 = jnp.bfloat16


def starts_of(index_values, lengths):
    ends = jnp.cumsum(lengths, dtype=jnp.int32)
    past = index_values[:, None] >= ends[None, :]
    return jnp.sum(jnp.where(past, lengths[None, :], 0), axis=1, dtype=jnp.int32)


def segment_of(index_values, lengths):
    ends = jnp.cumsum(lengths, dtype=jnp.int32)
    return jnp.sum((index_values[:, None] >= ends[None, :]).astype(jnp.int32), axis=1, dtype=jnp.int32)


def insert_map(text_rows, image_lengths, gaps):
    offsets = jnp.cumsum(image_lengths, dtype=jnp.int32) - image_lengths
    starts = jnp.cumsum(gaps, dtype=jnp.int32)[: image_lengths.shape[0]] + offsets
    inside = (text_rows[:, None] >= starts[None, :]) & (
        text_rows[:, None] < (starts + image_lengths)[None, :]
    )
    source = jnp.sum(
        jnp.where(inside, offsets[None, :] + text_rows[:, None] - starts[None, :], 0),
        axis=1,
        dtype=jnp.int32,
    )
    return (source, jnp.any(inside, axis=1))


class Links:
    def __init__(self, send, recv, rows, cols):
        self.send, self.recv = send, recv
        self.rows, self.cols = rows, cols
        self.r, self.c = lax.axis_index("row"), lax.axis_index("col")
        self.g = lax.axis_index("grp")
        self.high, self.low = self.r // 2, self.r % 2
        self.count = 0
        self.taken = 0
        self.pending = []

    def slots(self, number):
        base = self.taken
        self.taken += number
        return base

    def push(self, src, dst, slot, **where):
        copy = pltpu.make_async_remote_copy(
            src_ref=src,
            dst_ref=dst,
            send_sem=self.send.at[self.count],
            recv_sem=self.recv.at[slot],
            device_id=where,
            device_id_type=pl.DeviceIdType.MESH,
        )
        self.count += 1
        copy.start()
        self.pending.append(copy)

    def arrived(self, dst, slot):
        pltpu.make_async_remote_copy(
            src_ref=dst,
            dst_ref=dst,
            send_sem=self.send.at[0],
            recv_sem=self.recv.at[slot],
            device_id={"row": self.r},
            device_id_type=pl.DeviceIdType.MESH,
        ).wait_recv()

    def row_peer(self, step):
        return (self.high + step) % (self.rows // 2) * 2 + self.low

    def row_start(self, src, dst, base):
        other = self.high * 2 + 1 - self.low
        for step in range(1, self.rows // 2):
            self.push(src, dst.at[self.r], base + self.r, row=self.row_peer(step))
        self.push(src, dst.at[self.r], base + self.r, row=other)

    def row_forward(self, dst, base):
        other = self.high * 2 + 1 - self.low
        for step in range(1, self.rows // 2):
            at = self.row_peer(self.rows // 2 - step)
            self.arrived(dst.at[at], base + at)
            self.push(dst.at[at], dst.at[at], base + at, row=other)

    def row_finish(self, dst, base):
        for step in range(self.rows // 2):
            at = (self.high + step) % (self.rows // 2) * 2 + 1 - self.low
            self.arrived(dst.at[at], base + at)

    def col_start(self, src, dst, base):
        for step in range(1, self.cols):
            self.push(src, dst, base + self.c, col=(self.c + step) % self.cols)

    def col_finish(self, dst, base):
        for step in range(1, self.cols):
            at = (self.c + step) % self.cols
            self.arrived(dst.at[at], base + at)


def front_kernel(
    patch_ref, small_ref, wv_in, wvb_ref, ids_ref, idk_ref, vo_in, vob_ref, proj_ref, projb_ref,
    gain_in, wd_in, meta_in, *rest,
    texts, rows, cols, hr, scale, width,
):
    text_in, rest = rest[:texts], rest[texts:]
    (q_ref, kv_ref, imgq_ref, imgkv_ref, image_ref, meta_ref, x_ref, s_ref, wv_ref, vo_ref, wd_ref,
     gain_ref, at_ref, part_ref, send, recv, local), text_ref = rest[:17], rest[17:]
    net = Links(send, recv, rows, cols)
    r, c, g = net.r, net.c, net.g
    k_out = vo_in.shape[1] // 2
    k_dec = wd_in.shape[1] // 2
    vo_half = pl.ds(pl.multiple_of(g * k_out, 16), k_out)
    vo_rest = pl.ds(pl.multiple_of((1 - g) * k_out, 16), k_out)
    wd_half = pl.ds(pl.multiple_of(g * k_dec, 16), k_dec)
    wd_rest = pl.ds(pl.multiple_of((1 - g) * k_dec, 16), k_dec)
    barrier = pltpu.get_barrier_semaphore()
    for step in range(1, rows):
        pl.semaphore_signal(barrier, inc=1, device_id={"row": (r + step) % rows},
                            device_id_type=pl.DeviceIdType.MESH)
    for step in range(1, cols):
        pl.semaphore_signal(barrier, inc=1, device_id={"col": (c + step) % cols},
                            device_id_type=pl.DeviceIdType.MESH)
    pl.semaphore_signal(barrier, inc=1, device_id={"grp": 1 - g},
                        device_id_type=pl.DeviceIdType.MESH)
    pl.semaphore_wait(barrier, rows + cols - 1)

    own = [
        (patch_ref, x_ref.at[c, r]),
        (small_ref, s_ref.at[c]),
        (wv_in.at[c * hr // cols], wv_ref.at[c]),
        (vo_in.at[:, vo_half], vo_ref.at[r, :, vo_half]),
        (wd_in.at[r, wd_half], wd_ref.at[r, wd_half]),
        (gain_in, gain_ref.at[r]),
        (meta_in, meta_ref.at[g]),
    ]
    own += [(a, b.at[c, r]) for a, b in zip(text_in, text_ref)]
    own = [pltpu.make_async_copy(a, b, local.at[i]) for i, (a, b) in enumerate(own)]
    for copy in own:
        copy.start()

    x_row, x_col = net.slots(rows), net.slots(cols)
    s_col, wv_col = net.slots(cols), net.slots(cols)
    vo_row, wd_row, gain_row = net.slots(rows), net.slots(rows), net.slots(rows)
    text_row = [net.slots(rows) for _ in text_in]
    text_col = [net.slots(cols) for _ in text_in]
    at_row, at_col = net.slots(rows), net.slots(cols)
    part_col, img_row, meta_grp = net.slots(cols), net.slots(rows), net.slots(1)
    kv_grp, imgkv_grp = net.slots(cols), net.slots(1)
    vo_grp, wd_grp = net.slots(1), net.slots(1)

    net.row_start(patch_ref, x_ref.at[c], x_row)
    net.col_start(small_ref, s_ref.at[c], s_col)
    for step in range(1, cols):
        to = (c + step) % cols
        net.push(wv_in.at[to * hr // cols], wv_ref.at[c], wv_col + c, col=to)
    net.push(meta_in, meta_ref.at[g], meta_grp, grp=1 - g)
    net.row_start(gain_in, gain_ref, gain_row)
    net.row_start(vo_in.at[:, vo_half], vo_ref.at[:, :, vo_half], vo_row)
    for step in range(1, rows):
        to = (r + step) % rows
        net.push(wd_in.at[to, wd_half], wd_ref.at[r, wd_half], wd_row + r, row=to)
    for copy in own:
        copy.wait()
    net.row_forward(x_ref.at[c], x_row)
    net.row_finish(x_ref.at[c], x_row)
    net.col_start(x_ref.at[c], x_ref.at[c], x_col)
    net.col_finish(s_ref, s_col)
    net.col_finish(wv_ref, wv_col)
    net.col_finish(x_ref, x_col)

    count = rows * patch_ref.shape[0]
    depth = patch_ref.shape[1]
    one = jnp.zeros((count, 1), F32)
    two = jnp.zeros((count, 1), F32)
    for i in range(cols):
        x = x_ref[i].reshape(count, depth).astype(F32)
        one += jnp.sum(x, axis=1, keepdims=True)
        two += jnp.sum(x * x, axis=1, keepdims=True)
    mean = one / width
    inv = lax.rsqrt(two / width - mean * mean + 1e-06)
    qkv = jnp.zeros((count, 3 * PAD), F32)
    for i in range(cols):
        x = x_ref[i].reshape(count, depth).astype(F32)
        normed = ((x - mean) * inv * s_ref[i, 0:1] + s_ref[i, 1:2]).astype(BF16)
        qkv += jnp.dot(normed, wv_ref[i], preferred_element_type=F32)
    qkv = (qkv + wvb_ref[...].astype(F32)).astype(BF16)
    q, k, v = qkv[:, :PAD], qkv[:, PAD : 2 * PAD], qkv[:, 2 * PAD :]
    scores = lax.dot_general(q, k, (((1,), (1,)), ((), ())), preferred_element_type=F32)
    scores = scores * (scale * LOG2E)
    allowed = ids_ref[...] == idk_ref[...]
    scores = jnp.where(allowed, scores, -1e30)
    top = jnp.max(scores, axis=1, keepdims=True)
    weights = jnp.where(allowed, jnp.exp2(scores - top), 0.0)
    total = jnp.sum(weights, axis=1, keepdims=True)
    mixed = jnp.dot(weights.astype(BF16), v, preferred_element_type=F32) / total
    mine = c * hr // cols
    at_ref[mine, r] = mixed.astype(BF16)
    net.row_start(at_ref.at[mine, r], at_ref.at[mine], at_row)
    for a, b, base in zip(text_in, text_ref, text_row):
        net.row_start(a, b.at[c], base)
    net.row_forward(vo_ref.at[:, :, vo_half], vo_row)
    net.row_finish(vo_ref.at[:, :, vo_half], vo_row)
    net.push(vo_ref.at[:, :, vo_half], vo_ref.at[:, :, vo_half], vo_grp, grp=1 - g)
    net.row_forward(at_ref.at[mine], at_row)
    net.row_finish(at_ref.at[mine], at_row)
    for step in range(1, hr):
        to = (c + step * (cols // hr)) % cols
        net.push(at_ref.at[mine], at_ref.at[mine], at_col + mine, col=to)
    for step in range(1, rows):
        at = (r + step) % rows
        net.arrived(wd_ref.at[at, wd_half], wd_row + at)
    net.push(wd_ref.at[:, wd_half], wd_ref.at[:, wd_half], wd_grp, grp=1 - g)
    net.arrived(vo_ref.at[:, :, vo_rest], vo_grp)
    for step in range(1, hr):
        other = (mine + step) % hr
        net.arrived(at_ref.at[other], at_col + other)

    delta = x_ref[c].reshape(count, depth).astype(F32) + vob_ref[...].astype(F32)
    for i in range(rows):
        for h in range(hr):
            delta += jnp.dot(
                at_ref[h, i][:, : 2 * k_out], vo_ref[i, h], preferred_element_type=F32
            )
    tokens = count // 4
    resid = delta.astype(BF16).reshape(rows, 4, tokens // rows, depth)
    partial = jnp.zeros(part_ref.shape[1:], F32)
    for i in range(4):
        quarter = resid[:, i].reshape(tokens, depth)
        partial += jnp.dot(quarter, proj_ref[i], preferred_element_type=F32)
    part_ref[c] = partial
    net.col_start(part_ref.at[c], part_ref.at[c], part_col)
    net.col_finish(part_ref, part_col)
    image = projb_ref[...].astype(F32)
    for i in range(cols):
        image = image + part_ref[i]
    image_ref[r] = image.astype(BF16)
    net.row_start(image_ref.at[r], image_ref, img_row)
    net.row_forward(gain_ref, gain_row)
    net.row_finish(gain_ref, gain_row)
    for b, base in zip(text_ref, text_row):
        net.row_forward(b.at[c], base)
    for b, base, other in zip(text_ref, text_row, text_col):
        net.row_finish(b.at[c], base)
        net.col_start(b.at[c], b.at[c], other)
    net.row_forward(image_ref, img_row)
    net.arrived(wd_ref.at[:, wd_rest], wd_grp)

    def head_rows(part):
        number = part(0).shape[0]
        squares = jnp.zeros((number, 1), F32)
        for i in range(rows):
            x = part(i).astype(F32)
            squares += jnp.sum(x * x, axis=1, keepdims=True)
        inv = lax.rsqrt(squares / width + 1e-05)
        total = jnp.zeros((number, 3 * PAD), F32)
        for i in range(rows):
            normed = (part(i).astype(F32) * inv * gain_ref[i, 0:1]).astype(BF16)
            total += jnp.dot(normed, wd_ref[i], preferred_element_type=F32)
        return total.astype(BF16)

    own_rows = sum(b.shape[2] for b in text_ref[:2])

    def text_block(at):
        for piece in range(2):
            @pl.loop(0, own_rows // 2 // TPD)
            def _(j):
                take = pl.ds(pl.multiple_of(j * TPD, TPD), TPD)

                def part(i):
                    x = text_ref[piece][at, i, take]
                    if len(text_ref) < 3:
                        return x
                    tail = text_ref[2][at, i, take]
                    return jnp.concatenate([x, tail[:, piece * 64 : piece * 64 + 64]], axis=1)

                found = head_rows(part)
                put = at * own_rows + piece * (own_rows // 2) + j * TPD
                put = pl.ds(pl.multiple_of(put, TPD), TPD)
                q_ref[put] = found[:, :PAD]
                kv_ref[g, put] = found[:, PAD:]
        rows_of = pl.ds(pl.multiple_of(at * own_rows, TPD), own_rows)
        net.push(kv_ref.at[g, rows_of], kv_ref.at[g, rows_of], kv_grp + at, grp=1 - g)

    text_block(c)
    net.row_finish(image_ref, img_row)
    found = head_rows(lambda i: image_ref[i])
    imgq_ref[...] = found[:, :PAD]
    imgkv_ref[g] = found[:, PAD:]
    net.push(imgkv_ref.at[g], imgkv_ref.at[g], imgkv_grp, grp=1 - g)
    for b, base in zip(text_ref, text_col):
        net.col_finish(b, base)
    for step in range(1, cols):
        text_block((c + step) % cols)
    net.arrived(meta_ref.at[1 - g], meta_grp)
    net.arrived(imgkv_ref.at[1 - g], imgkv_grp)
    for step in range(cols):
        at = (c + step) % cols
        rows_of = pl.ds(pl.multiple_of(at * own_rows, TPD), own_rows)
        net.arrived(kv_ref.at[1 - g, rows_of], kv_grp + at)
    for copy in net.pending:
        copy.wait_send()


def front(patch, small, wv, wvb, ids, vo, vob, proj, projb, texts, gain, wd, meta, rows, cols, scale):
    hr = wv.shape[0]
    count = rows * patch.shape[0]
    half = cols * 2 * texts[0].shape[0]
    number = len(texts)
    tokens = count // 4
    depth = proj.shape[2]
    args = (patch, small, wv, wvb, ids[:, None], ids[None, :], vo, vob, proj, projb, gain, wd, meta) + tuple(texts)
    sends = (6 + number) * (rows - 1) + (5 + number) * (cols - 1) + 4 + cols
    slots = (6 + number) * rows + (5 + number) * cols + 4 + cols
    vmem = pl.BlockSpec(memory_space=pltpu.VMEM)
    return pl.pallas_call(
        functools.partial(
            front_kernel, texts=number, rows=rows, cols=cols, hr=hr, scale=scale,
            width=HEADS * HEAD_DIM,
        ),
        in_specs=[vmem] * len(args),
        out_specs=[vmem] * 6,
        out_shape=[
            jax.ShapeDtypeStruct((half, PAD), BF16),
            jax.ShapeDtypeStruct((2, half, 2 * PAD), BF16),
            jax.ShapeDtypeStruct((tokens, PAD), BF16),
            jax.ShapeDtypeStruct((2, tokens, 2 * PAD), BF16),
            jax.ShapeDtypeStruct((rows, tokens, depth), BF16),
            jax.ShapeDtypeStruct((2,) + meta.shape, jnp.int32),
        ],
        scratch_shapes=[
            pltpu.VMEM((cols, rows) + patch.shape, BF16),
            pltpu.VMEM((cols,) + small.shape, F32),
            pltpu.VMEM((cols,) + wv.shape[1:], BF16),
            pltpu.VMEM((rows,) + vo.shape, BF16),
            pltpu.VMEM(wd.shape, BF16),
            pltpu.VMEM((rows,) + gain.shape, F32),
            pltpu.VMEM((hr, rows, count, PAD), BF16),
            pltpu.VMEM((cols, tokens, depth), F32),
            pltpu.SemaphoreType.DMA((sends,)),
            pltpu.SemaphoreType.DMA((slots,)),
            pltpu.SemaphoreType.DMA((7 + number,)),
        ]
        + [pltpu.VMEM((cols, rows) + text.shape, BF16) for text in texts],
        compiler_params=pltpu.CompilerParams(
            collective_id=0, has_side_effects=True, vmem_limit_bytes=56 << 20
        ),
        name="front",
    )(*args)


def dec_attn_kernel(low_ref, q_ref, start_ref, pos_ref, k_ref, v_ref, o_ref, *, scale):
    b = pl.program_id(0)
    q = q_ref[...]
    begin = start_ref[...]
    at = pos_ref[...]
    count = q.shape[0]
    chunk = 2 * TPD

    def step(j, carry):
        best, norm, accum = carry
        rows = pl.ds(pl.multiple_of(j * TPD, TPD), TPD)
        k = jnp.concatenate([k_ref[0, rows], k_ref[1, rows]], axis=0)
        v = jnp.concatenate([v_ref[0, rows], v_ref[1, rows]], axis=0)
        scores = lax.dot_general(q, k, (((1,), (1,)), ((), ())), preferred_element_type=F32)
        scores = scores * (scale * LOG2E)
        key_at = j * chunk + lax.broadcasted_iota(jnp.int32, (count, chunk), 1)
        allowed = (key_at >= begin) & (key_at <= at)
        scores = jnp.where(allowed, scores, -1e30)
        new_best = jnp.maximum(best, jnp.max(scores, axis=1, keepdims=True))
        weights = jnp.where(allowed, jnp.exp2(scores - new_best), 0.0)
        factor = jnp.exp2(best - new_best)
        norm = norm * factor + jnp.sum(weights, axis=1, keepdims=True)
        accum = accum * factor + jnp.dot(weights.astype(BF16), v, preferred_element_type=F32)
        return new_best, norm, accum

    init = (
        jnp.full((count, 1), -1e30, F32),
        jnp.zeros((count, 1), F32),
        jnp.zeros((count, PAD), F32),
    )
    best, norm, accum = lax.fori_loop(low_ref[b], b + 1, step, init)
    o_ref[...] = (accum / norm).astype(BF16)


def dec_attn(q, k, v, begin, at, scale):
    count = q.shape[0]
    low = begin[::TPD] // (2 * TPD)
    return pl.pallas_call(
        functools.partial(dec_attn_kernel, scale=scale),
        grid_spec=pltpu.PrefetchScalarGridSpec(
            num_scalar_prefetch=1,
            grid=(count // TPD,),
            in_specs=[
                pl.BlockSpec((TPD, PAD), lambda i, s: (i, 0)),
                pl.BlockSpec((TPD, 1), lambda i, s: (i, 0)),
                pl.BlockSpec((TPD, 1), lambda i, s: (i, 0)),
                pl.BlockSpec(k.shape, lambda i, s: (0, 0, 0)),
                pl.BlockSpec(v.shape, lambda i, s: (0, 0, 0)),
            ],
            out_specs=pl.BlockSpec((TPD, PAD), lambda i, s: (i, 0)),
        ),
        out_shape=jax.ShapeDtypeStruct((count, PAD), BF16),
        compiler_params=pltpu.CompilerParams(vmem_limit_bytes=48 << 20),
        name="dec_attn",
    )(low, q, begin[:, None], at[:, None], k, v)


def pad_parts(w):
    lead = w.shape[:-1]
    w = w.reshape(lead + (3, HEAD_DIM))
    w = jnp.pad(w, [(0, 0)] * (len(lead) + 1) + [(0, PAD - HEAD_DIM)])
    return w.reshape(lead + (3 * PAD,))


def per_device(
    patches,
    vis_gain,
    vis_bias,
    vis_qkv,
    vis_qkv_bias,
    vis_out,
    vis_out_bias,
    proj_weight,
    proj_bias,
    text_embeds,
    dec_gain,
    dec_qkv,
    dec_out,
    image_tokens,
    text_gaps,
    doc_lengths,
):
    scale = HEAD_DIM ** (-0.5)
    C = lax.axis_size("col")
    R = lax.axis_size("row")
    c = lax.axis_index("col")
    r = lax.axis_index("row")
    g = lax.axis_index("grp")
    hr = HEADS // R
    hc = HEADS // C
    share = R // hc
    image_lengths = image_tokens[0]
    gaps = text_gaps[0]
    text = text_embeds[0]
    half_rows = text.shape[0] * C
    own_text = text.shape[0]

    dec_out_all = lax.all_gather(dec_out, ("col", "row"), axis=0)
    dec_out_all = dec_out_all.reshape((C, R) + dec_out.shape)
    patch_total = R * patches.shape[1]
    head_of = c * hr // C
    small = jnp.pad(jnp.stack([vis_gain, vis_bias]).astype(F32), ((0, 6), (0, 0)))
    wv = pad_parts(jnp.transpose(vis_qkv.reshape(-1, hr, 3 * HEAD_DIM), (1, 0, 2)))
    wvb = lax.dynamic_slice_in_dim(vis_qkv_bias, head_of * 3 * HEAD_DIM, 3 * HEAD_DIM, 0)
    wvb = pad_parts(wvb)[None]
    vo = jnp.pad(vis_out.reshape(hr, HEAD_DIM, -1), ((0, 0), (0, 96 - HEAD_DIM), (0, 0)))
    wd = jnp.transpose(dec_qkv.reshape(dec_qkv.shape[0], hc, 3 * HEAD_DIM), (1, 0, 2))
    wd = pad_parts(jnp.repeat(wd, share, axis=0) if share > 1 else wd)
    depth = text.shape[1]
    split = own_text // 2
    wide = PAD if depth <= PAD else PAD + 64
    more = wide - depth
    wd = jnp.pad(wd, ((0, 0), (0, more), (0, 0)))
    gain = jnp.pad(dec_gain.astype(F32)[None], ((0, 7), (0, more)))
    proj = jnp.pad(proj_weight, ((0, 0), (0, 0), (0, more)))
    projb = jnp.pad(proj_bias, (0, more))
    if depth <= PAD:
        filled = jnp.pad(text, ((0, 0), (0, more)))
        texts = [filled[:split], filled[split:]]
    else:
        tail = jnp.pad(text[:, PAD:], ((0, 0), (0, more)))
        texts = [text[:split, :PAD], text[split:, :PAD]]
        texts.append(jnp.concatenate([tail[:split], tail[split:]], axis=1))
    images = image_tokens.shape[1]
    meta = jnp.concatenate([image_lengths, gaps])
    meta = jnp.pad(meta[None], ((0, 7), (0, PAD - meta.shape[0])))
    patch = patches[0].reshape(-1, 4, patches.shape[2])
    patch = jnp.transpose(patch, (1, 0, 2)).reshape(patches.shape[1:])
    patch_ids = segment_of(jnp.arange(patch_total // 4, dtype=jnp.int32), image_lengths)
    patch_ids = jnp.tile(patch_ids.reshape(R, 1, -1), (1, 4, 1)).reshape(patch_total)
    q_text, kv_text, q_image, kv_image, image_all, meta = front(
        patch, small, wv, wvb, patch_ids, vo, vis_out_bias[None], proj,
        projb[None], texts, gain, wd, meta, R, C, scale,
    )
    image_rows = lax.dynamic_index_in_dim(image_all, r, 0, keepdims=False)[:, :depth]

    t = jnp.arange(half_rows, dtype=jnp.int32)

    def hot_of(lengths, spaces):
        source, inside = insert_map(t, lengths, spaces)
        pick = jnp.where(inside, source, -1)
        hot = pick[:, None] == jnp.arange(image_rows.shape[0], dtype=jnp.int32)[None]
        return hot.astype(BF16), inside

    hot, inside = hot_of(image_lengths, gaps)
    merged = []
    for half in range(2):
        hot_half, inside_half = hot_of(
            meta[half, 0, :images], meta[half, 0, images : 2 * images + 1]
        )
        placed = jnp.dot(hot_half, kv_image[half], preferred_element_type=F32).astype(BF16)
        merged.append(jnp.where(inside_half[:, None], placed, kv_text[half]))
    both = jnp.stack(merged)
    placed = jnp.dot(hot, q_image, preferred_element_type=F32).astype(BF16)
    query = jnp.where(inside[:, None], placed, q_text)
    at = t // TPD * (2 * TPD) + g * TPD + t % TPD
    begin = starts_of(at, doc_lengths)
    out = dec_attn(query, both[..., :PAD], both[..., PAD:], begin, at, scale)

    mine = half_rows // (C * R)
    spread = out[:, :HEAD_DIM].reshape(C * R, mine, HEAD_DIM)
    rows = lax.all_to_all(spread, ("col", "row"), 0, 0)
    rows = rows.reshape(C, R, mine, HEAD_DIM)[:, ::share]
    rows = jnp.transpose(rows, (0, 2, 1, 3)).reshape(C, mine, hc * HEAD_DIM)
    delta = jnp.einsum(
        "ctk,crkf->rtf", rows, dec_out_all, preferred_element_type=F32
    ).astype(BF16)
    delta = lax.all_to_all(delta, "row", 0, 0).reshape(own_text, text.shape[1])
    own_hot = lax.dynamic_slice_in_dim(hot, c * own_text, own_text, 0)
    own_inside = lax.dynamic_slice_in_dim(inside, c * own_text, own_text, 0)
    own_placed = jnp.dot(own_hot, image_rows, preferred_element_type=F32)
    dec_input = jnp.where(own_inside[:, None], own_placed, text.astype(F32))
    return (dec_input + delta.astype(F32)).astype(BF16)[None]


def solution(mesh):
    return jax.shard_map(
        per_device,
        mesh=mesh,
        in_specs=(
            P("grp", "row", "col"),
            P("col"),
            P("col"),
            P("col", "row"),
            P("row"),
            P("row", "col"),
            P("col"),
            P(None, "col", "row"),
            P("row"),
            P("grp", "col", "row"),
            P("row"),
            P("row", "col"),
            P("col", "row"),
            P("grp", None),
            P("grp", None),
            P(),
        ),
        out_specs=P("grp", "col", "row"),
        check_vma=False,
    )
```

```python
import functools

import jax
import jax.numpy as jnp
from jax import lax
from jax.experimental import pallas as pl
from jax.experimental.pallas import tpu as pltpu
from jax.sharding import PartitionSpec as P

HEADS = 16
HEAD_DIM = 88
PAD = 128
TPD = 256
LOG2E = 1.4426950408889634
F32 = jnp.float32
BF16 = jnp.bfloat16


def starts_of(index_values, lengths):
    ends = jnp.cumsum(lengths, dtype=jnp.int32)
    past = index_values[:, None] >= ends[None, :]
    return jnp.sum(jnp.where(past, lengths[None, :], 0), axis=1, dtype=jnp.int32)


def segment_of(index_values, lengths):
    ends = jnp.cumsum(lengths, dtype=jnp.int32)
    return jnp.sum((index_values[:, None] >= ends[None, :]).astype(jnp.int32), axis=1, dtype=jnp.int32)


def insert_map(text_rows, image_lengths, gaps):
    offsets = jnp.cumsum(image_lengths, dtype=jnp.int32) - image_lengths
    starts = jnp.cumsum(gaps, dtype=jnp.int32)[: image_lengths.shape[0]] + offsets
    inside = (text_rows[:, None] >= starts[None, :]) & (
        text_rows[:, None] < (starts + image_lengths)[None, :]
    )
    source = jnp.sum(
        jnp.where(inside, offsets[None, :] + text_rows[:, None] - starts[None, :], 0),
        axis=1,
        dtype=jnp.int32,
    )
    return (source, jnp.any(inside, axis=1))


class Links:
    def __init__(self, send, recv, rows, cols):
        self.send, self.recv = send, recv
        self.rows, self.cols = rows, cols
        self.r, self.c = lax.axis_index("row"), lax.axis_index("col")
        self.g = lax.axis_index("grp")
        self.high, self.low = self.r // 2, self.r % 2
        self.count = 0
        self.taken = 0
        self.pending = []

    def slots(self, number):
        base = self.taken
        self.taken += number
        return base

    def push(self, src, dst, slot, **where):
        copy = pltpu.make_async_remote_copy(
            src_ref=src,
            dst_ref=dst,
            send_sem=self.send.at[self.count],
            recv_sem=self.recv.at[slot],
            device_id=where,
            device_id_type=pl.DeviceIdType.MESH,
        )
        self.count += 1
        copy.start()
        self.pending.append(copy)

    def arrived(self, dst, slot):
        pltpu.make_async_remote_copy(
            src_ref=dst,
            dst_ref=dst,
            send_sem=self.send.at[0],
            recv_sem=self.recv.at[slot],
            device_id={"row": self.r},
            device_id_type=pl.DeviceIdType.MESH,
        ).wait_recv()

    def row_peer(self, step):
        return (self.high + step) % (self.rows // 2) * 2 + self.low

    def row_start(self, src, dst, base):
        other = self.high * 2 + 1 - self.low
        for step in range(1, self.rows // 2):
            self.push(src, dst.at[self.r], base + self.r, row=self.row_peer(step))
        self.push(src, dst.at[self.r], base + self.r, row=other)

    def row_forward(self, dst, base):
        other = self.high * 2 + 1 - self.low
        for step in range(1, self.rows // 2):
            at = self.row_peer(self.rows // 2 - step)
            self.arrived(dst.at[at], base + at)
            self.push(dst.at[at], dst.at[at], base + at, row=other)

    def row_finish(self, dst, base):
        for step in range(self.rows // 2):
            at = (self.high + step) % (self.rows // 2) * 2 + 1 - self.low
            self.arrived(dst.at[at], base + at)

    def col_start(self, src, dst, base):
        for step in range(1, self.cols):
            self.push(src, dst, base + self.c, col=(self.c + step) % self.cols)

    def col_finish(self, dst, base):
        for step in range(1, self.cols):
            at = (self.c + step) % self.cols
            self.arrived(dst.at[at], base + at)


def front_kernel(
    patch_ref, small_ref, wv_in, wvb_ref, ids_ref, idk_ref, vo_in, vob_ref, proj_ref, projb_ref,
    gain_in, wd_in, meta_in, *rest,
    texts, rows, cols, hr, scale, width,
):
    text_in, rest = rest[:texts], rest[texts:]
    (q_ref, kv_ref, imgq_ref, imgkv_ref, image_ref, meta_ref, x_ref, s_ref, wv_ref, vo_ref, wd_ref,
     gain_ref, at_ref, part_ref, send, recv, local), text_ref = rest[:17], rest[17:]
    net = Links(send, recv, rows, cols)
    r, c, g = net.r, net.c, net.g
    k_out = vo_in.shape[1] // 2
    k_dec = wd_in.shape[1] // 2
    vo_half = pl.ds(pl.multiple_of(g * k_out, 16), k_out)
    vo_rest = pl.ds(pl.multiple_of((1 - g) * k_out, 16), k_out)
    wd_half = pl.ds(pl.multiple_of(g * k_dec, 16), k_dec)
    wd_rest = pl.ds(pl.multiple_of((1 - g) * k_dec, 16), k_dec)
    barrier = pltpu.get_barrier_semaphore()
    for step in range(1, rows):
        pl.semaphore_signal(barrier, inc=1, device_id={"row": (r + step) % rows},
                            device_id_type=pl.DeviceIdType.MESH)
    for step in range(1, cols):
        pl.semaphore_signal(barrier, inc=1, device_id={"col": (c + step) % cols},
                            device_id_type=pl.DeviceIdType.MESH)
    pl.semaphore_signal(barrier, inc=1, device_id={"grp": 1 - g},
                        device_id_type=pl.DeviceIdType.MESH)
    pl.semaphore_wait(barrier, rows + cols - 1)

    own = [
        (patch_ref, x_ref.at[c, r]),
        (small_ref, s_ref.at[c]),
        (wv_in.at[c * hr // cols], wv_ref.at[c]),
        (vo_in.at[:, vo_half], vo_ref.at[r, :, vo_half]),
        (wd_in.at[r, wd_half], wd_ref.at[r, wd_half]),
        (gain_in, gain_ref.at[r]),
        (meta_in, meta_ref.at[g]),
    ]
    own += [(a, b.at[c, r]) for a, b in zip(text_in, text_ref)]
    own = [pltpu.make_async_copy(a, b, local.at[i]) for i, (a, b) in enumerate(own)]
    for copy in own:
        copy.start()

    x_row, x_col = net.slots(rows), net.slots(cols)
    s_col, wv_col = net.slots(cols), net.slots(cols)
    vo_row, wd_row, gain_row = net.slots(rows), net.slots(rows), net.slots(rows)
    text_row = [net.slots(rows) for _ in text_in]
    text_col = [net.slots(cols) for _ in text_in]
    at_row, at_col = net.slots(rows), net.slots(cols)
    part_col, img_row, meta_grp = net.slots(cols), net.slots(rows), net.slots(1)
    kv_grp, imgkv_grp = net.slots(2 * cols), net.slots(1)
    vo_grp, wd_grp = net.slots(1), net.slots(1)

    net.row_start(patch_ref, x_ref.at[c], x_row)
    net.col_start(small_ref, s_ref.at[c], s_col)
    for step in range(1, cols):
        to = (c + step) % cols
        net.push(wv_in.at[to * hr // cols], wv_ref.at[c], wv_col + c, col=to)
    net.push(meta_in, meta_ref.at[g], meta_grp, grp=1 - g)
    net.row_start(gain_in, gain_ref, gain_row)
    net.row_start(vo_in.at[:, vo_half], vo_ref.at[:, :, vo_half], vo_row)
    for step in range(1, rows):
        to = (r + step) % rows
        net.push(wd_in.at[to, wd_half], wd_ref.at[r, wd_half], wd_row + r, row=to)
    for copy in own:
        copy.wait()
    net.row_forward(x_ref.at[c], x_row)
    net.row_finish(x_ref.at[c], x_row)
    net.col_start(x_ref.at[c], x_ref.at[c], x_col)
    net.col_finish(s_ref, s_col)
    net.col_finish(wv_ref, wv_col)
    net.col_finish(x_ref, x_col)

    count = rows * patch_ref.shape[0]
    depth = patch_ref.shape[1]
    one = jnp.zeros((count, 1), F32)
    two = jnp.zeros((count, 1), F32)
    for i in range(cols):
        x = x_ref[i].reshape(count, depth).astype(F32)
        one += jnp.sum(x, axis=1, keepdims=True)
        two += jnp.sum(x * x, axis=1, keepdims=True)
    mean = one / width
    inv = lax.rsqrt(two / width - mean * mean + 1e-06)
    qkv = jnp.zeros((count, 3 * PAD), F32)
    for i in range(cols):
        x = x_ref[i].reshape(count, depth).astype(F32)
        normed = ((x - mean) * inv * s_ref[i, 0:1] + s_ref[i, 1:2]).astype(BF16)
        qkv += jnp.dot(normed, wv_ref[i], preferred_element_type=F32)
    qkv = (qkv + wvb_ref[...].astype(F32)).astype(BF16)
    q, k, v = qkv[:, :PAD], qkv[:, PAD : 2 * PAD], qkv[:, 2 * PAD :]
    scores = lax.dot_general(q, k, (((1,), (1,)), ((), ())), preferred_element_type=F32)
    scores = scores * (scale * LOG2E)
    allowed = ids_ref[...] == idk_ref[...]
    scores = jnp.where(allowed, scores, -1e30)
    top = jnp.max(scores, axis=1, keepdims=True)
    weights = jnp.where(allowed, jnp.exp2(scores - top), 0.0)
    total = jnp.sum(weights, axis=1, keepdims=True)
    mixed = jnp.dot(weights.astype(BF16), v, preferred_element_type=F32) / total
    mine = c * hr // cols
    at_ref[mine, r] = mixed.astype(BF16)
    net.row_start(at_ref.at[mine, r], at_ref.at[mine], at_row)
    for a, b, base in zip(text_in, text_ref, text_row):
        net.row_start(a, b.at[c], base)
    net.row_forward(vo_ref.at[:, :, vo_half], vo_row)
    net.row_finish(vo_ref.at[:, :, vo_half], vo_row)
    net.push(vo_ref.at[:, :, vo_half], vo_ref.at[:, :, vo_half], vo_grp, grp=1 - g)
    net.row_forward(at_ref.at[mine], at_row)
    net.row_finish(at_ref.at[mine], at_row)
    for step in range(1, hr):
        to = (c + step * (cols // hr)) % cols
        net.push(at_ref.at[mine], at_ref.at[mine], at_col + mine, col=to)
    for step in range(1, rows):
        at = (r + step) % rows
        net.arrived(wd_ref.at[at, wd_half], wd_row + at)
    net.push(wd_ref.at[:, wd_half], wd_ref.at[:, wd_half], wd_grp, grp=1 - g)
    net.row_forward(text_ref[0].at[c], text_row[0])
    net.arrived(vo_ref.at[:, :, vo_rest], vo_grp)
    for step in range(1, hr):
        other = (mine + step) % hr
        net.arrived(at_ref.at[other], at_col + other)

    delta = x_ref[c].reshape(count, depth).astype(F32) + vob_ref[...].astype(F32)
    for i in range(rows):
        for h in range(hr):
            delta += jnp.dot(
                at_ref[h, i][:, : 2 * k_out], vo_ref[i, h], preferred_element_type=F32
            )
    tokens = count // 4
    resid = delta.astype(BF16).reshape(rows, 4, tokens // rows, depth)
    partial = jnp.zeros(part_ref.shape[1:], F32)
    for i in range(4):
        quarter = resid[:, i].reshape(tokens, depth)
        partial += jnp.dot(quarter, proj_ref[i], preferred_element_type=F32)
    part_ref[c] = partial
    net.col_start(part_ref.at[c], part_ref.at[c], part_col)
    net.row_forward(text_ref[1].at[c], text_row[1])
    net.col_finish(part_ref, part_col)
    image = projb_ref[...].astype(F32)
    for i in range(cols):
        image = image + part_ref[i]
    image_ref[r] = image.astype(BF16)
    net.row_start(image_ref.at[r], image_ref, img_row)
    net.row_forward(gain_ref, gain_row)
    net.row_finish(gain_ref, gain_row)
    for b, base in zip(text_ref[2:], text_row[2:]):
        net.row_forward(b.at[c], base)
    for b, base, other in zip(text_ref, text_row, text_col):
        net.row_finish(b.at[c], base)
        net.col_start(b.at[c], b.at[c], other)
    net.row_forward(image_ref, img_row)
    net.arrived(wd_ref.at[:, wd_rest], wd_grp)

    def head_rows(part):
        number = part(0).shape[0]
        squares = jnp.zeros((number, 1), F32)
        for i in range(rows):
            x = part(i).astype(F32)
            squares += jnp.sum(x * x, axis=1, keepdims=True)
        inv = lax.rsqrt(squares / width + 1e-05)
        total = jnp.zeros((number, 3 * PAD), F32)
        for i in range(rows):
            normed = (part(i).astype(F32) * inv * gain_ref[i, 0:1]).astype(BF16)
            total += jnp.dot(normed, wd_ref[i], preferred_element_type=F32)
        return total.astype(BF16)

    own_rows = sum(b.shape[2] for b in text_ref[:2])

    def piece_rows(at, piece):
        first = at * own_rows + piece * (own_rows // 2)
        return pl.ds(pl.multiple_of(first, TPD), own_rows // 2)

    def text_block(at):
        for piece in range(2):
            @pl.loop(0, own_rows // 2 // TPD)
            def _(j):
                take = pl.ds(pl.multiple_of(j * TPD, TPD), TPD)

                def part(i):
                    x = text_ref[piece][at, i, take]
                    if len(text_ref) < 3:
                        return x
                    tail = text_ref[2][at, i, take]
                    return jnp.concatenate([x, tail[:, piece * 64 : piece * 64 + 64]], axis=1)

                found = head_rows(part)
                put = at * own_rows + piece * (own_rows // 2) + j * TPD
                put = pl.ds(pl.multiple_of(put, TPD), TPD)
                q_ref[put] = found[:, :PAD]
                kv_ref[g, put] = found[:, PAD:]
            rows_of = piece_rows(at, piece)
            sent = kv_ref.at[g, rows_of]
            net.push(sent, sent, kv_grp + 2 * at + piece, grp=1 - g)

    text_block(c)
    net.row_finish(image_ref, img_row)
    found = head_rows(lambda i: image_ref[i])
    imgq_ref[...] = found[:, :PAD]
    imgkv_ref[g] = found[:, PAD:]
    net.push(imgkv_ref.at[g], imgkv_ref.at[g], imgkv_grp, grp=1 - g)
    for b, base in zip(text_ref, text_col):
        net.col_finish(b, base)
    for step in range(1, cols):
        text_block((c + step) % cols)
    net.arrived(meta_ref.at[1 - g], meta_grp)
    net.arrived(imgkv_ref.at[1 - g], imgkv_grp)
    for step in range(cols):
        at = (c + step) % cols
        for piece in range(2):
            net.arrived(kv_ref.at[1 - g, piece_rows(at, piece)], kv_grp + 2 * at + piece)
    for copy in net.pending:
        copy.wait_send()


def front(patch, small, wv, wvb, ids, vo, vob, proj, projb, texts, gain, wd, meta, rows, cols, scale):
    hr = wv.shape[0]
    count = rows * patch.shape[0]
    half = cols * 2 * texts[0].shape[0]
    number = len(texts)
    tokens = count // 4
    depth = proj.shape[2]
    args = (patch, small, wv, wvb, ids[:, None], ids[None, :], vo, vob, proj, projb, gain, wd, meta) + tuple(texts)
    sends = (6 + number) * (rows - 1) + (5 + number) * (cols - 1) + 4 + 2 * cols
    slots = (6 + number) * rows + (5 + number) * cols + 4 + 2 * cols
    vmem = pl.BlockSpec(memory_space=pltpu.VMEM)
    return pl.pallas_call(
        functools.partial(
            front_kernel, texts=number, rows=rows, cols=cols, hr=hr, scale=scale,
            width=HEADS * HEAD_DIM,
        ),
        in_specs=[vmem] * len(args),
        out_specs=[vmem] * 6,
        out_shape=[
            jax.ShapeDtypeStruct((half, PAD), BF16),
            jax.ShapeDtypeStruct((2, half, 2 * PAD), BF16),
            jax.ShapeDtypeStruct((tokens, PAD), BF16),
            jax.ShapeDtypeStruct((2, tokens, 2 * PAD), BF16),
            jax.ShapeDtypeStruct((rows, tokens, depth), BF16),
            jax.ShapeDtypeStruct((2,) + meta.shape, jnp.int32),
        ],
        scratch_shapes=[
            pltpu.VMEM((cols, rows) + patch.shape, BF16),
            pltpu.VMEM((cols,) + small.shape, F32),
            pltpu.VMEM((cols,) + wv.shape[1:], BF16),
            pltpu.VMEM((rows,) + vo.shape, BF16),
            pltpu.VMEM(wd.shape, BF16),
            pltpu.VMEM((rows,) + gain.shape, F32),
            pltpu.VMEM((hr, rows, count, PAD), BF16),
            pltpu.VMEM((cols, tokens, depth), F32),
            pltpu.SemaphoreType.DMA((sends,)),
            pltpu.SemaphoreType.DMA((slots,)),
            pltpu.SemaphoreType.DMA((7 + number,)),
        ]
        + [pltpu.VMEM((cols, rows) + text.shape, BF16) for text in texts],
        compiler_params=pltpu.CompilerParams(
            collective_id=0, has_side_effects=True, vmem_limit_bytes=56 << 20
        ),
        name="front",
    )(*args)


def dec_attn_kernel(low_ref, q_ref, start_ref, pos_ref, k_ref, v_ref, o_ref, *, scale):
    b = pl.program_id(0)
    q = q_ref[...]
    begin = start_ref[...]
    at = pos_ref[...]
    count = q.shape[0]
    chunk = 2 * TPD

    def step(j, carry):
        best, norm, accum = carry
        rows = pl.ds(pl.multiple_of(j * TPD, TPD), TPD)
        k = jnp.concatenate([k_ref[0, rows], k_ref[1, rows]], axis=0)
        v = jnp.concatenate([v_ref[0, rows], v_ref[1, rows]], axis=0)
        scores = lax.dot_general(q, k, (((1,), (1,)), ((), ())), preferred_element_type=F32)
        scores = scores * (scale * LOG2E)
        key_at = j * chunk + lax.broadcasted_iota(jnp.int32, (count, chunk), 1)
        allowed = (key_at >= begin) & (key_at <= at)
        scores = jnp.where(allowed, scores, -1e30)
        new_best = jnp.maximum(best, jnp.max(scores, axis=1, keepdims=True))
        weights = jnp.where(allowed, jnp.exp2(scores - new_best), 0.0)
        factor = jnp.exp2(best - new_best)
        norm = norm * factor + jnp.sum(weights, axis=1, keepdims=True)
        accum = accum * factor + jnp.dot(weights.astype(BF16), v, preferred_element_type=F32)
        return new_best, norm, accum

    init = (
        jnp.full((count, 1), -1e30, F32),
        jnp.zeros((count, 1), F32),
        jnp.zeros((count, PAD), F32),
    )
    best, norm, accum = lax.fori_loop(low_ref[b], b + 1, step, init)
    o_ref[...] = (accum / norm).astype(BF16)


def dec_attn(q, k, v, begin, at, scale):
    count = q.shape[0]
    low = begin[::TPD] // (2 * TPD)
    return pl.pallas_call(
        functools.partial(dec_attn_kernel, scale=scale),
        grid_spec=pltpu.PrefetchScalarGridSpec(
            num_scalar_prefetch=1,
            grid=(count // TPD,),
            in_specs=[
                pl.BlockSpec((TPD, PAD), lambda i, s: (i, 0)),
                pl.BlockSpec((TPD, 1), lambda i, s: (i, 0)),
                pl.BlockSpec((TPD, 1), lambda i, s: (i, 0)),
                pl.BlockSpec(k.shape, lambda i, s: (0, 0, 0)),
                pl.BlockSpec(v.shape, lambda i, s: (0, 0, 0)),
            ],
            out_specs=pl.BlockSpec((TPD, PAD), lambda i, s: (i, 0)),
        ),
        out_shape=jax.ShapeDtypeStruct((count, PAD), BF16),
        compiler_params=pltpu.CompilerParams(vmem_limit_bytes=48 << 20),
        name="dec_attn",
    )(low, q, begin[:, None], at[:, None], k, v)


def pad_parts(w):
    lead = w.shape[:-1]
    w = w.reshape(lead + (3, HEAD_DIM))
    w = jnp.pad(w, [(0, 0)] * (len(lead) + 1) + [(0, PAD - HEAD_DIM)])
    return w.reshape(lead + (3 * PAD,))


def per_device(
    patches,
    vis_gain,
    vis_bias,
    vis_qkv,
    vis_qkv_bias,
    vis_out,
    vis_out_bias,
    proj_weight,
    proj_bias,
    text_embeds,
    dec_gain,
    dec_qkv,
    dec_out,
    image_tokens,
    text_gaps,
    doc_lengths,
):
    scale = HEAD_DIM ** (-0.5)
    C = lax.axis_size("col")
    R = lax.axis_size("row")
    c = lax.axis_index("col")
    r = lax.axis_index("row")
    g = lax.axis_index("grp")
    hr = HEADS // R
    hc = HEADS // C
    share = R // hc
    image_lengths = image_tokens[0]
    gaps = text_gaps[0]
    text = text_embeds[0]
    half_rows = text.shape[0] * C
    own_text = text.shape[0]

    dec_out_all = lax.all_gather(dec_out, ("col", "row"), axis=0)
    dec_out_all = dec_out_all.reshape((C, R) + dec_out.shape)
    patch_total = R * patches.shape[1]
    head_of = c * hr // C
    small = jnp.pad(jnp.stack([vis_gain, vis_bias]).astype(F32), ((0, 6), (0, 0)))
    wv = pad_parts(jnp.transpose(vis_qkv.reshape(-1, hr, 3 * HEAD_DIM), (1, 0, 2)))
    wvb = lax.dynamic_slice_in_dim(vis_qkv_bias, head_of * 3 * HEAD_DIM, 3 * HEAD_DIM, 0)
    wvb = pad_parts(wvb)[None]
    vo = jnp.pad(vis_out.reshape(hr, HEAD_DIM, -1), ((0, 0), (0, 96 - HEAD_DIM), (0, 0)))
    wd = jnp.transpose(dec_qkv.reshape(dec_qkv.shape[0], hc, 3 * HEAD_DIM), (1, 0, 2))
    wd = pad_parts(jnp.repeat(wd, share, axis=0) if share > 1 else wd)
    depth = text.shape[1]
    split = own_text // 2
    wide = PAD if depth <= PAD else PAD + 64
    more = wide - depth
    wd = jnp.pad(wd, ((0, 0), (0, more), (0, 0)))
    gain = jnp.pad(dec_gain.astype(F32)[None], ((0, 7), (0, more)))
    proj = jnp.pad(proj_weight, ((0, 0), (0, 0), (0, more)))
    projb = jnp.pad(proj_bias, (0, more))
    if depth <= PAD:
        filled = jnp.pad(text, ((0, 0), (0, more)))
        texts = [filled[:split], filled[split:]]
    else:
        tail = jnp.pad(text[:, PAD:], ((0, 0), (0, more)))
        texts = [text[:split, :PAD], text[split:, :PAD]]
        texts.append(jnp.concatenate([tail[:split], tail[split:]], axis=1))
    images = image_tokens.shape[1]
    meta = jnp.concatenate([image_lengths, gaps])
    meta = jnp.pad(meta[None], ((0, 7), (0, PAD - meta.shape[0])))
    patch = patches[0].reshape(-1, 4, patches.shape[2])
    patch = jnp.transpose(patch, (1, 0, 2)).reshape(patches.shape[1:])
    patch_ids = segment_of(jnp.arange(patch_total // 4, dtype=jnp.int32), image_lengths)
    patch_ids = jnp.tile(patch_ids.reshape(R, 1, -1), (1, 4, 1)).reshape(patch_total)
    q_text, kv_text, q_image, kv_image, image_all, meta = front(
        patch, small, wv, wvb, patch_ids, vo, vis_out_bias[None], proj,
        projb[None], texts, gain, wd, meta, R, C, scale,
    )
    image_rows = lax.dynamic_index_in_dim(image_all, r, 0, keepdims=False)[:, :depth]

    t = jnp.arange(half_rows, dtype=jnp.int32)

    def hot_of(lengths, spaces):
        source, inside = insert_map(t, lengths, spaces)
        pick = jnp.where(inside, source, -1)
        hot = pick[:, None] == jnp.arange(image_rows.shape[0], dtype=jnp.int32)[None]
        return hot.astype(BF16), inside

    hot, inside = hot_of(image_lengths, gaps)
    merged = []
    for half in range(2):
        hot_half, inside_half = hot_of(
            meta[half, 0, :images], meta[half, 0, images : 2 * images + 1]
        )
        placed = jnp.dot(hot_half, kv_image[half], preferred_element_type=F32).astype(BF16)
        merged.append(jnp.where(inside_half[:, None], placed, kv_text[half]))
    both = jnp.stack(merged)
    placed = jnp.dot(hot, q_image, preferred_element_type=F32).astype(BF16)
    query = jnp.where(inside[:, None], placed, q_text)
    at = t // TPD * (2 * TPD) + g * TPD + t % TPD
    begin = starts_of(at, doc_lengths)
    out = dec_attn(query, both[..., :PAD], both[..., PAD:], begin, at, scale)

    mine = half_rows // (C * R)
    spread = out[:, :HEAD_DIM].reshape(C * R, mine, HEAD_DIM)
    rows = lax.all_to_all(spread, ("col", "row"), 0, 0)
    rows = rows.reshape(C, R, mine, HEAD_DIM)[:, ::share]
    rows = jnp.transpose(rows, (0, 2, 1, 3)).reshape(C, mine, hc * HEAD_DIM)
    delta = jnp.einsum(
        "ctk,crkf->rtf", rows, dec_out_all, preferred_element_type=F32
    ).astype(BF16)
    delta = lax.all_to_all(delta, "row", 0, 0).reshape(own_text, text.shape[1])
    own_hot = lax.dynamic_slice_in_dim(hot, c * own_text, own_text, 0)
    own_inside = lax.dynamic_slice_in_dim(inside, c * own_text, own_text, 0)
    own_placed = jnp.dot(own_hot, image_rows, preferred_element_type=F32)
    dec_input = jnp.where(own_inside[:, None], own_placed, text.astype(F32))
    return (dec_input + delta.astype(F32)).astype(BF16)[None]


def solution(mesh):
    return jax.shard_map(
        per_device,
        mesh=mesh,
        in_specs=(
            P("grp", "row", "col"),
            P("col"),
            P("col"),
            P("col", "row"),
            P("row"),
            P("row", "col"),
            P("col"),
            P(None, "col", "row"),
            P("row"),
            P("grp", "col", "row"),
            P("row"),
            P("row", "col"),
            P("col", "row"),
            P("grp", None),
            P("grp", None),
            P(),
        ),
        out_specs=P("grp", "col", "row"),
        check_vma=False,
    )
```
